256 devices in a mesh: role: 2 (over core), grp: 16 (over x, y), tp: 8 (over z).
Axes of the slice: x: 4, y: 4, z: 8, core: 2. Of those that a mesh axis runs over, the one named last changes fastest.
Arguments:
- queries: bfloat16 [2, 512, 6144], P('role', 'grp', 'tp'), may hold values from -7 to 7
- new_keys: bfloat16 [2, 512, 1024], P('role', 'grp', 'tp'), may hold values from -4 to 4
- new_values: bfloat16 [2, 512, 1024], P('role', 'grp', 'tp'), may hold values from -4 to 4
- cache_keys: bfloat16 [2, 512, 8, 256, 128], P('role', 'grp', 'tp'), may hold values from -4 to 4
- cache_values: bfloat16 [2, 512, 8, 256, 128], P('role', 'grp', 'tp'), may hold values from -4 to 4
- lengths: int32 [2, 512], P('role', 'grp'), may hold values from 1 to 256, as said below
- out_proj: bfloat16 [6144, 6144], P('tp', 'grp'), may hold values from -0.25 to 0.25
- residual: bfloat16 [2, 512, 6144], P('role', None, 'grp'), may hold values from -14 to 14
- norm_gain: float32 [6144], replicated, may hold values from 0.1 to 1.9
- expert_ids: int32 [2, 512, 2], replicated, may hold values from 0 to 7, all different within a row; in each aligned block of 512 rows (0 to 511, 512 to 1023, ..., all dimensions but the last counted through in order) at most 256 rows name the same one
- gate_weights: float32 [2, 512, 2], replicated, may hold values from 0.25 to 1
- expert_gate: bfloat16 [8, 6144, 8192], P('tp', None, ('role', 'grp')), may hold values from -0.078125 to 0.078125
- expert_up: bfloat16 [8, 6144, 8192], P('tp', None, ('role', 'grp')), may hold values from -0.078125 to 0.078125
- expert_down: bfloat16 [8, 8192, 6144], P('tp', 'role', 'grp'), may hold values from -0.0625 to 0.0625
Outputs:
- stream: bfloat16 [2, 512, 6144], P('role', None, 'grp')
- expert_mix: bfloat16 [2, 512, 6144], P('role', None, 'grp')
The draws below stay inside these ranges and needn't reach their ends.
Inputs may be any that keep to these rules, and one draw needn't show every extreme that they name: `expert_ids`: the two experts of a token differ. Among the tokens of one micro-batch no expert is named more than 256 times, and in some micro-batch some expert is named exactly 256 times. `lengths`: cache positions at or past a sequence's length hold no data of it. Every micro-batch has a sequence of length 256.
All inputs are finite; a program needn't handle non-finite values.
Results may differ from the reference program's by a relative error of at most 0.02.
Values may be sent and summed in bfloat16 or wider, within the bound.
A program may use at most 128 MiB of HBM per device.

```python
import math
import jax
import jax.numpy as jnp
import numpy as np
from jax import lax

MICRO = 2
LEN = 256
D = 6144
QH = 48
KVH = 8
HD = 128
EXPERTS = 8
FF = 8192
SEQS = 512
CAP = 256


def draw_queries(key, part):
    key = jax.random.fold_in(key, 11)
    shape = (MICRO, SEQS, QH, HD)
    values = jax.random.truncated_normal(key, -4.0, 4.0, shape, jnp.float32)
    return values.reshape(MICRO, SEQS, QH * HD).astype(jnp.bfloat16)


def draw_new_keys(key, part):
    key = jax.random.fold_in(key, 13)
    shape = (MICRO, SEQS, KVH, HD)
    values = jax.random.truncated_normal(key, -4.0, 4.0, shape, jnp.float32)
    return values.reshape(MICRO, SEQS, KVH * HD).astype(jnp.bfloat16)


def draw_cache_keys(key, part):
    key = jax.random.fold_in(key, 17)
    shape = (MICRO, SEQS, KVH, LEN, HD)
    return jax.random.truncated_normal(key, -4.0, 4.0, shape, jnp.float32).astype(jnp.bfloat16)


def draw_lengths(key, part):
    key = jax.random.fold_in(key, 19)
    first, second = jax.random.split(key)
    drawn = jax.random.randint(first, (MICRO, SEQS), 1, LEN + 1)
    chosen = jax.random.randint(second, (MICRO, 1), 0, SEQS)
    return jnp.where(jnp.arange(SEQS)[None, :] == chosen, LEN, drawn).astype(jnp.int32)


def draw_residual(key, part):
    key = jax.random.fold_in(key, 23)
    column = jnp.arange(D, dtype=jnp.float32) / (D - 1)
    scale = 0.35 * jnp.power(10.0, column)
    return (jax.random.truncated_normal(key, -4.0, 4.0, (MICRO, SEQS, D), jnp.float32) * scale).astype(jnp.bfloat16)


def levels(own_key, dims, shards, least, top_value):
    def one(dim, parts):
        steps = jax.random.uniform(jax.random.fold_in(jax.random.fold_in(own_key, 6), dim), (parts,), jnp.float32, least / len(shards), top_value / len(shards))
        return jnp.repeat(jnp.exp(steps), dims[dim] // parts).reshape((-1,) + (1,) * (len(dims) - dim - 1))

    level = one(*shards[0])
    for cut in shards[1:]:
        level = level * one(*cut)
    return level


def deal_out(rng, own, number, rows, amount, top, bound, slope):
    ranking = jax.random.permutation(rng, amount)
    packed, usual = load_shares(amount, rows * top, bound, slope, True), load_shares(amount, rows * top, bound, slope, False)
    places = jnp.arange(amount)

    def named(sizes, rotation):
        used = int((sizes > 0).sum())
        fixed = max(1, used // 4)
        moved = fixed + (places - fixed + rotation * (used - fixed)) % max(1, amount - fixed)
        return jnp.zeros((amount,), jnp.int32).at[ranking[jnp.where(places < fixed, places, moved)]].set(jnp.asarray(sizes, jnp.int32))

    sizes = jnp.where(number % 4 == 0, named(packed, number // 4), named(usual, number - number // 4 - 1))
    mixed = jax.random.permutation(jax.random.fold_in(own, 3), amount)
    donor, receiver = mixed[0:amount // 2 * 2:2], mixed[1:amount // 2 * 2:2]
    room = jnp.minimum(sizes[donor] - 1, bound - sizes[receiver]) // 2
    room = jnp.where((donor == ranking[0]) | (receiver == ranking[0]) | (sizes[receiver] == 0), 0, jnp.maximum(room, 0))
    moved = jax.random.randint(jax.random.fold_in(own, 4), (amount // 2,), 0, 1 << 20) % (room + 1)
    sizes = sizes.at[donor].add(-moved).at[receiver].add(moved)
    items = jnp.searchsorted(jnp.cumsum(sizes), jnp.arange(rows * top), side="right").astype(jnp.int32)
    table = items.reshape(top, rows).T
    table = table[jax.random.permutation(jax.random.fold_in(own, 1), rows)]
    rotation = jax.random.randint(jax.random.fold_in(own, 2), (rows, 1), 0, top)
    return jnp.take_along_axis(table, (jnp.arange(top)[None, :] + rotation) % top, axis=1)


def load_shares(count, total, reach, skew, full):
    loads = [(1 << 20) // math.isqrt(rank ** skew) + 1 for rank in range(1, count + 1)]
    largest = reach if full else min(reach, max(-(-total // count), total * loads[0] // sum(loads)))
    least = 1 if total - largest >= count - 1 else 0
    holding, rest = [largest] + [least] * (count - 1), total - largest - least * (count - 1)
    while rest > 0:
        candidates = [i for i in range(1, count) if holding[i] < largest] or [i for i in range(1, count) if holding[i] < reach]
        whole, budget = sum([loads[i] for i in candidates]), rest
        for i in candidates:
            extra = min(reach - holding[i], max(1, budget * loads[i] // whole), rest)
            holding[i] = holding[i] + extra
            rest = rest - extra
    return np.array(holding)


def gaussian(stream_key, extent, deviation, reach, pieces=(), held_as=jnp.bfloat16):
    loudness = levels(stream_key, extent, pieces, -0.22, 0.18) if pieces else 1.0
    array = jax.random.normal(stream_key, extent, jnp.float32) * deviation * loudness
    return jnp.minimum(jnp.maximum(array, -reach), reach).astype(held_as)


def setup_inputs(seed: int = 0) -> dict:
    arg_keys = jax.random.split(jax.random.key(seed), 15)
    queries = draw_queries(jax.random.fold_in(arg_keys[14], 71), 0)
    new_keys = draw_new_keys(jax.random.fold_in(arg_keys[14], 71), 0)
    new_values = gaussian(arg_keys[2], (MICRO, SEQS, KVH * HD), 1.0, 4.0, ((0, 2), (1, 16), (2, 8)))
    cache_keys = draw_cache_keys(jax.random.fold_in(arg_keys[14], 71), 0)
    cache_values = gaussian(arg_keys[4], (MICRO, SEQS, KVH, LEN, HD), 1.0, 4.0, ((0, 2), (1, 16), (2, 8)))
    lengths = draw_lengths(jax.random.fold_in(arg_keys[14], 71), 0)
    out_proj = gaussian(arg_keys[6], (D, D), (4 * HD) ** -0.5, 0.25, ((0, 8), (1, 16)))
    residual = draw_residual(jax.random.fold_in(arg_keys[14], 71), 0)
    norm_gain = jnp.clip(1.0 + 0.18 * jax.random.normal(arg_keys[8], (D,), jnp.float32), 0.1, 1.9)
    expert_ids_keys = jax.random.split(jax.random.fold_in(arg_keys[9], 1), MICRO * SEQS // SEQS)
    expert_ids_turns = jax.random.permutation(jax.random.fold_in(arg_keys[9], 3), MICRO * SEQS // SEQS)
    expert_ids = jax.vmap(lambda own, number: deal_out(jax.random.fold_in(arg_keys[9], 2), own, number, SEQS, EXPERTS, 2, CAP, 2))(expert_ids_keys, expert_ids_turns).reshape((MICRO, SEQS, 2))
    gate_weights = jnp.clip(jax.random.uniform(arg_keys[10], (MICRO, SEQS, 2), jnp.float32, 0.25, 1.0), 0.25, 1.0)
    expert_gate = gaussian(arg_keys[11], (EXPERTS, D, FF), D ** -0.5, 0.078125, ((0, 8), (2, 32)))
    expert_up = gaussian(arg_keys[12], (EXPERTS, D, FF), D ** -0.5, 0.078125, ((0, 8), (2, 32)))
    expert_down = gaussian(arg_keys[13], (EXPERTS, FF, D), FF ** -0.5, 0.0625, ((0, 8), (1, 2), (2, 16)))
    return {"queries": queries, "new_keys": new_keys, "new_values": new_values, "cache_keys": cache_keys, "cache_values": cache_values, "lengths": lengths, "out_proj": out_proj, "residual": residual, "norm_gain": norm_gain, "expert_ids": expert_ids, "gate_weights": gate_weights, "expert_gate": expert_gate, "expert_up": expert_up, "expert_down": expert_down}


def attend_micro(query, fresh_key, fresh_value, keys, values, length):
    group = QH // KVH
    factor = 1.0 / math.sqrt(HD)
    query = query.reshape(SEQS, KVH, group, HD).astype(jnp.float32)
    fresh_key = fresh_key.reshape(SEQS, KVH, HD).astype(jnp.float32)
    fresh_value = fresh_value.reshape(SEQS, KVH, HD).astype(jnp.float32)
    scores = jnp.einsum('skgd,skpd->skgp', query, keys.astype(jnp.float32)) * factor
    fresh = jnp.einsum('skgd,skd->skg', query, fresh_key) * factor
    valid = (jnp.arange(LEN, dtype=jnp.int32)[None, :] < length[:, None])[:, None, None, :]
    scores = jnp.where(valid, scores, -jnp.inf)
    highest = jnp.maximum(lax.optimization_barrier(jnp.max(scores, axis=-1)), fresh)
    weights = jnp.exp(scores - highest[..., None])
    own = jnp.exp(fresh - highest)
    denominator = lax.optimization_barrier(jnp.sum(weights, axis=-1)) + own
    probs = (weights / denominator[..., None]).astype(jnp.bfloat16).astype(jnp.float32)
    own_prob = (own / denominator).astype(jnp.bfloat16).astype(jnp.float32)
    mixed = jnp.einsum('skgp,skpd->skgd', probs, values.astype(jnp.float32))
    mixed = mixed + own_prob[..., None] * fresh_value[:, :, None, :]
    return mixed.reshape(SEQS, QH * HD).astype(jnp.bfloat16)

def reference(queries, new_keys, new_values, cache_keys, cache_values, lengths, out_proj, residual, norm_gain, expert_ids, gate_weights, expert_gate, expert_up, expert_down):
    attn = lax.map(lambda entry: attend_micro(*entry), (queries, new_keys, new_values, cache_keys, cache_values, lengths))
    head_out = jnp.dot(attn.reshape(MICRO * SEQS, D), out_proj, preferred_element_type=jnp.float32).reshape(MICRO, SEQS, D)
    stream = (residual.astype(jnp.float32) + head_out).astype(jnp.bfloat16)
    wide = stream.astype(jnp.float32)
    rstat = 1.0 / jnp.sqrt(lax.optimization_barrier(jnp.mean(wide * wide, axis=-1)) + 1e-05)
    scaled = (wide * norm_gain).astype(jnp.bfloat16)
    routed = expert_ids.reshape(MICRO, SEQS * 2)
    weight_flat = gate_weights.reshape(MICRO, SEQS * 2)
    onehot = (routed[:, :, None] == jnp.arange(EXPERTS, dtype=jnp.int32)[None, None, :]).astype(jnp.int32)
    before = jnp.cumsum(onehot, axis=1) - onehot
    position = lax.optimization_barrier(jnp.sum(before * onehot, axis=2))
    token_index = jnp.arange(SEQS * 2, dtype=jnp.int32) // 2

    def one_expert(carry, entry):
        gate_matrix, up_matrix, down_matrix, expert = entry
        picked = (routed[:, None, :] == expert) & (position[:, None, :] == jnp.arange(CAP, dtype=jnp.int32)[None, :, None])
        which = lax.optimization_barrier(jnp.sum(jnp.where(picked, token_index[None, None, :], 0), axis=2)).astype(jnp.int32)
        weight = lax.optimization_barrier(jnp.sum(jnp.where(picked, weight_flat[:, None, :], 0.0), axis=2))
        chosen = jax.vmap(lambda table, where_rows: table[where_rows])(scaled, which).reshape(MICRO * CAP, D)
        factor = jax.vmap(lambda table, where_rows: table[where_rows])(rstat, which).reshape(MICRO * CAP, 1)
        gate_act = factor * jnp.dot(chosen, gate_matrix, preferred_element_type=jnp.float32)
        up_act = factor * jnp.dot(chosen, up_matrix, preferred_element_type=jnp.float32)
        hidden = (jax.nn.silu(gate_act) * up_act).astype(jnp.bfloat16)
        produced = jnp.dot(hidden, down_matrix, preferred_element_type=jnp.float32).reshape(MICRO, CAP, D)
        placed = jax.vmap(lambda rows_out, where_rows, scale_rows: jax.ops.segment_sum(rows_out * scale_rows[:, None], where_rows, num_segments=SEQS))(produced, which, weight)
        return (carry + placed, None)
    mix, _ = lax.scan(one_expert, jnp.zeros((MICRO, SEQS, D), jnp.float32), (expert_gate, expert_up, expert_down, jnp.arange(EXPERTS, dtype=jnp.int32)))
    return (stream, mix.astype(jnp.bfloat16))
```

```python
import math

import jax
import jax.numpy as jnp
from jax import lax
from jax.experimental import pallas as pl
from jax.experimental.pallas import tpu as pltpu
from jax.sharding import PartitionSpec as P

MESH = pl.DeviceIdType.MESH
BF16 = jnp.bfloat16
F32 = jnp.float32
D = 6144
SIDE = 4
GROUPS = 16
PLANES = 8


def attend_local(queries, new_keys, new_values, cache_keys, cache_values, lengths):
    seqs = cache_keys.shape[1]
    kv_heads = cache_keys.shape[2]
    span = cache_keys.shape[3]
    head_dim = cache_keys.shape[4]
    group = queries.shape[2] // (kv_heads * head_dim)
    factor = 1.0 / math.sqrt(head_dim)
    query = queries[0].reshape(seqs, kv_heads, group, head_dim)
    fresh_key = new_keys[0].reshape(seqs, kv_heads, head_dim)
    fresh_value = new_values[0].reshape(seqs, kv_heads, head_dim)
    scores = (
        jnp.einsum("skgd,skpd->skgp", query, cache_keys[0], preferred_element_type=jnp.float32)
        * factor
    )
    fresh = (
        jnp.einsum("skgd,skd->skg", query, fresh_key, preferred_element_type=jnp.float32) * factor
    )
    valid = (jnp.arange(span, dtype=jnp.int32)[None, :] < lengths[0][:, None])[:, None, None, :]
    scores = jnp.where(valid, scores, -jnp.inf)
    highest = jnp.maximum(jnp.max(scores, axis=-1), fresh)
    weights = jnp.exp(scores - highest[..., None])
    own = jnp.exp(fresh - highest)
    denominator = jnp.sum(weights, axis=-1) + own
    probs = (weights / denominator[..., None]).astype(jnp.bfloat16)
    own_prob = (own / denominator).astype(jnp.bfloat16)
    mixed = jnp.einsum(
        "skgp,skpd->skgd", probs, cache_values[0], preferred_element_type=jnp.float32
    )
    mixed = (
        mixed
        + own_prob.astype(jnp.float32)[..., None] * fresh_value.astype(jnp.float32)[:, :, None, :]
    )
    return mixed.reshape(seqs, group * kv_heads * head_dim).astype(jnp.bfloat16)


def remote(src, dst, send_sem, recv_sem, device):
    return pltpu.make_async_remote_copy(
        src_ref=src,
        dst_ref=dst,
        send_sem=send_sem,
        recv_sem=recv_sem,
        device_id=device,
        device_id_type=MESH,
    )


class PlaneGather:
    def __init__(self, place, piece, send, recv):
        self.place, self.piece, self.send, self.recv = place, piece, send, recv

    def at(self, half, first, second):
        role, x, y, plane = self.place
        dx, dy = (first, second) if half == 0 else (second, first)
        return lax.rem(x + dx, SIDE) * SIDE + lax.rem(y + dy, SIDE)

    def copy(self, half, first, phase, step):
        role, x, y, plane = self.place
        piece = self.piece(self.at(half, first, 0), half)
        if phase == 0:
            target = self.at(half, step, 0)
            send, recv = self.send.at[half, SIDE, step], self.recv.at[half, SIDE - step, 0]
        else:
            target = self.at(half, 0, step)
            send, recv = self.send.at[half, first, step], self.recv.at[half, first, SIDE - step]
        return remote(piece, piece, send, recv, (role, target, plane))

    def wait(self, half, first, second):
        role, x, y, plane = self.place
        piece = self.piece(self.at(half, first, second), half)
        remote(
            piece, piece, self.send.at[half, 0, 0], self.recv.at[half, first, second], (role, 0, plane)
        ).wait_recv()

    def start(self, halves=(0, 1)):
        for step in (1, 3, 2):
            for half in halves:
                self.copy(half, 0, 0, step).start()
        for step in (1, 3, 2):
            for half in halves:
                self.copy(half, 0, 1, step).start()

    def forward(self):
        for first in (1, 3, 2):
            for half in (0, 1):
                self.wait(half, first, 0)
                for step in (1, 3, 2):
                    self.copy(half, first, 1, step).start()

    def finish(self):
        def body(step, carry):
            for half in (0, 1):
                self.copy(half, 0, 0, step).wait_send()
                for first in range(SIDE):
                    self.copy(half, first, 1, step).wait_send()
            return carry

        lax.fori_loop(1, SIDE, body, 0)


def layer(
    attn_ref,
    proj_hbm,
    resid_ref,
    gain_ref,
    ids_ref,
    gates_ref,
    gate_hbm,
    up_hbm,
    down_hbm,
    stream_ref,
    mix_ref,
    attn_all,
    proj,
    gate_w,
    up_w,
    down_w,
    heads,
    head_in,
    rows_all,
    gate_acc,
    up_acc,
    square_acc,
    hidden_all,
    down_acc,
    half_out,
    half_in,
    mix_part,
    mix_in,
    pick,
    place_t,
    weight_col,
    load_sem,
    attn_send,
    attn_recv,
    rows_send,
    rows_recv,
    hid_send,
    hid_recv,
    sib_send,
    sib_recv,
    z_send,
    z_recv,
):
    role = lax.axis_index("role")
    grp = lax.axis_index("grp")
    plane = lax.axis_index("tp")
    x, y = grp // SIDE, lax.rem(grp, SIDE)
    place = (role, x, y, plane)
    sibling = (1 - role, grp, plane)

    def along_z(step):
        return (role, grp, lax.rem(plane + step, PLANES))

    loads = [
        pltpu.make_async_copy(src, dst, load_sem.at[i])
        for i, (src, dst) in enumerate(
            ((proj_hbm, proj), (gate_hbm, gate_w), (up_hbm, up_w), (down_hbm, down_w))
        )
    ]
    for load in loads:
        load.start()

    barrier = pltpu.get_barrier_semaphore()
    near = [(role, lax.rem(x + k, SIDE) * SIDE + y, plane) for k in (1, 2, 3)]
    near += [(role, x * SIDE + lax.rem(y + k, SIDE), plane) for k in (1, 2, 3)]
    near += [along_z(k) for k in range(1, PLANES)] + [sibling]
    for device in near:
        pl.semaphore_signal(barrier, inc=1, device_id=device, device_id_type=MESH)
    pl.semaphore_wait(barrier, len(near))

    attn_all[pl.ds(grp * 32, 32), :] = attn_ref[...]
    attn = PlaneGather(
        place, lambda g, half: attn_all.at[pl.ds(g * 32 + half * 16, 16)], attn_send, attn_recv
    )
    attn.start()

    ids = ids_ref[role]
    hit0, hit1 = ids[0:1, :] == plane, ids[1:2, :] == plane
    named = jnp.where(hit0 | hit1, 1.0, 0.0)
    gates = gates_ref[role]
    weight_row = jnp.where(hit0, gates[0:1, :], gates[1:2, :])
    seqs = named.shape[1]
    slots = pick.shape[0]
    earlier = lax.broadcasted_iota(jnp.int32, (seqs, seqs), 0) < lax.broadcasted_iota(
        jnp.int32, (seqs, seqs), 1
    )
    before = jnp.dot(
        jnp.broadcast_to(named, (16, seqs)).astype(BF16),
        jnp.where(earlier, 1.0, 0.0).astype(BF16),
        preferred_element_type=F32,
    )[0:1, :]
    slot = jnp.where(named > 0.5, before, -1.0).astype(jnp.int32)
    chosen = jnp.where(
        slot == lax.broadcasted_iota(jnp.int32, (slots, seqs), 0), 1.0, 0.0
    )
    pick[...] = chosen.astype(BF16)
    place_t[...] = chosen.T.astype(BF16)
    weight_col[...] = jnp.broadcast_to(
        jnp.sum(chosen * weight_row, axis=1, keepdims=True), weight_col.shape
    )
    gate_acc[...] = jnp.zeros_like(gate_acc)
    up_acc[...] = jnp.zeros_like(up_acc)
    square_acc[...] = jnp.zeros_like(square_acc)
    down_acc[...] = jnp.zeros_like(down_acc)

    attn.forward()

    def attn_rest(s, carry):
        attn.wait(0, 0, s)
        attn.wait(1, 0, s)
        for first in range(1, SIDE):
            attn.wait(0, first, s)
            attn.wait(1, first, s)
        return carry

    lax.fori_loop(1, SIDE, attn_rest, 0)
    loads[0].wait()

    def project(i, carry):
        part = jnp.dot(attn_all[pl.ds(i * 256, 256), :], proj[...], preferred_element_type=F32)
        heads[pl.ds(i * 256, 256), :] = part.astype(BF16)
        return carry

    lax.fori_loop(0, 2, project, 0)

    mine = pl.ds(plane * 64, 64)

    def scatter(src, dst, s):
        def one(step):
            to = lax.rem(plane + step, PLANES)
            return remote(
                src.at[pl.ds(to * 64, 64)],
                dst.at[step],
                z_send.at[s, step],
                z_recv.at[s, step],
                along_z(step),
            )

        def go(step, carry):
            one(step).start()
            return carry

        def arrive(step, carry):
            one(step).wait_recv()
            return carry + dst[step].astype(F32)

        lax.fori_loop(1, PLANES, go, 0)
        return lax.fori_loop(1, PLANES, arrive, src[mine, :].astype(F32)), one

    def spread(ref, s):
        def one(step, owner):
            block = ref.at[pl.ds(owner * 64, 64)]
            return remote(block, block, z_send.at[s, step], z_recv.at[s, step], along_z(step))

        def go(step, carry):
            one(step, plane).start()
            return carry

        def arrive(step, carry):
            one(step, lax.rem(plane + PLANES - step, PLANES)).wait_recv()
            return carry

        lax.fori_loop(1, PLANES, go, 0)
        lax.fori_loop(1, PLANES, arrive, 0)
        return lambda step: one(step, plane)

    summed, heads_copy = scatter(heads, head_in, 0)
    stream_ref[mine, :] = (resid_ref[mine, :].astype(F32) + summed).astype(BF16)
    stream_copy = spread(stream_ref, 1)

    gain = gain_ref[pl.ds(grp, 1), :]
    scaled = (stream_ref[...].astype(F32) * gain).astype(BF16)
    rows_all[role, grp] = jnp.dot(pick[...], scaled, preferred_element_type=F32).astype(BF16)
    rows = PlaneGather(
        place,
        lambda g, half: rows_all.at[role, g, pl.ds(half * 128, 128)],
        rows_send,
        rows_recv,
    )
    rows.start()

    def block_at(dx, dy):
        return lax.rem(x + dx, SIDE) * SIDE + lax.rem(y + dy, SIDE)

    def sibling_copy(dx, dy):
        block = rows_all.at[role, block_at(dx, dy)]
        return remote(block, block, sib_send.at[dx, dy], sib_recv.at[dx, dy], sibling)

    def sibling_wait(dx, dy):
        block = rows_all.at[1 - role, block_at(dx, dy)]
        remote(block, block, sib_send.at[dx, dy], sib_recv.at[dx, dy], sibling).wait_recv()

    sibling_copy(0, 0).start()
    loads[1].wait()
    loads[2].wait()

    def expert_in(dx, dy):
        g = block_at(dx, dy)
        depth = pl.ds(pl.multiple_of(g * 384, 128), 384)
        inverse = 1.0 / gain_ref[pl.ds(g, 1), :]
        for micro in range(2):
            block = rows_all[micro, g]
            into = pl.ds(micro * 256, 256)
            gate_acc[into, :] += jnp.dot(block, gate_w[depth, :], preferred_element_type=F32)
            up_acc[into, :] += jnp.dot(block, up_w[depth, :], preferred_element_type=F32)
            plain = block.astype(F32) * inverse
            plain = plain * plain
            square_acc[into, :] += plain[:, :128] + plain[:, 128:256] + plain[:, 256:]

    rows.forward()
    sibling_wait(0, 0)
    expert_in(0, 0)

    def row_axis(s, carry):
        rows.wait(1, 0, s)
        sibling_copy(s, 0).start()
        rows.wait(0, 0, s)
        sibling_copy(0, s).start()
        sibling_wait(s, 0)
        expert_in(s, 0)
        sibling_wait(0, s)
        expert_in(0, s)
        return carry

    lax.fori_loop(1, SIDE, row_axis, 0)

    def row_rest(s, carry):
        dx, dy = 1 + s // 3, 1 + lax.rem(s, 3)
        rows.wait(0, dx, dy)
        rows.wait(1, dy, dx)
        sibling_copy(dx, dy).start()
        sibling_wait(dx, dy)
        expert_in(dx, dy)
        return carry

    lax.fori_loop(0, 9, row_rest, 0)

    hid = PlaneGather(
        place, lambda g, half: hidden_all.at[g, pl.ds(half * 256, 256)], hid_send, hid_recv
    )
    for micro in range(2):
        into = pl.ds(micro * 256, 256)
        mean = jnp.sum(square_acc[into, :], axis=1, keepdims=True) / D
        rstat = 1.0 / jnp.sqrt(mean + 1e-05)
        act = gate_acc[into, :] * rstat
        hidden_all[grp, into, :] = (act / (1.0 + jnp.exp(-act)) * (up_acc[into, :] * rstat)).astype(
            BF16
        )
        hid.start((micro,))
    loads[3].wait()

    def expert_out(dx, dy):
        g = block_at(dx, dy)
        depth = pl.ds(pl.multiple_of(g * 256, 256), 256)
        for micro in range(2):
            into = pl.ds(micro * 256, 256)
            down_acc[into, :] += jnp.dot(
                hidden_all[g, into, :], down_w[depth, :], preferred_element_type=F32
            )

    hid.forward()
    expert_out(0, 0)

    def hid_axis(s, carry):
        hid.wait(1, 0, s)
        expert_out(s, 0)
        hid.wait(0, 0, s)
        expert_out(0, s)
        return carry

    lax.fori_loop(1, SIDE, hid_axis, 0)

    def hid_rest(s, carry):
        dx, dy = 1 + s // 3, 1 + lax.rem(s, 3)
        hid.wait(0, dx, dy)
        hid.wait(1, dy, dx)
        expert_out(dx, dy)
        return carry

    lax.fori_loop(0, 9, hid_rest, 0)

    half_out[...] = down_acc[pl.ds((1 - role) * 256, 256), :].astype(BF16)
    exchange = remote(half_out, half_in, sib_send.at[0, 4], sib_recv.at[0, 4], sibling)
    exchange.start()
    exchange.wait_recv()
    whole = down_acc[pl.ds(role * 256, 256), :] + half_in[...].astype(F32)
    weighted = (whole * weight_col[:, 0:1]).astype(BF16)
    mix_part[...] = jnp.dot(place_t[...], weighted, preferred_element_type=F32).astype(BF16)
    total, mix_copy = scatter(mix_part, mix_in, 2)
    mix_ref[mine, :] = total.astype(BF16)
    out_copy = spread(mix_ref, 3)

    attn.finish()
    rows.finish()
    hid.finish()
    exchange.wait_send()

    def sent_z(step, carry):
        heads_copy(step).wait_send()
        stream_copy(step).wait_send()
        mix_copy(step).wait_send()
        out_copy(step).wait_send()
        return carry

    lax.fori_loop(1, PLANES, sent_z, 0)

    def sent_sibling(s, carry):
        sibling_copy(s // SIDE, lax.rem(s, SIDE)).wait_send()
        return carry

    lax.fori_loop(0, GROUPS, sent_sibling, 0)


def local(
    queries,
    new_keys,
    new_values,
    cache_keys,
    cache_values,
    lengths,
    out_proj,
    residual,
    norm_gain,
    expert_ids,
    gate_weights,
    expert_gate,
    expert_up,
    expert_down,
):
    attn = attend_local(queries, new_keys, new_values, cache_keys, cache_values, lengths)
    vmem = pl.BlockSpec(memory_space=pltpu.VMEM)
    hbm = pl.BlockSpec(memory_space=pl.ANY)
    dma = pltpu.SemaphoreType.DMA
    stream, mix = pl.pallas_call(
        layer,
        out_shape=(
            jax.ShapeDtypeStruct((512, 384), BF16),
            jax.ShapeDtypeStruct((512, 384), BF16),
        ),
        in_specs=[vmem, hbm, vmem, vmem, vmem, vmem, hbm, hbm, hbm],
        out_specs=(vmem, vmem),
        scratch_shapes=[
            pltpu.VMEM((512, 768), BF16),
            pltpu.VMEM((768, 384), BF16),
            pltpu.VMEM((6144, 256), BF16),
            pltpu.VMEM((6144, 256), BF16),
            pltpu.VMEM((4096, 384), BF16),
            pltpu.VMEM((512, 384), BF16),
            pltpu.VMEM((8, 64, 384), BF16),
            pltpu.VMEM((2, 16, 256, 384), BF16),
            pltpu.VMEM((512, 256), F32),
            pltpu.VMEM((512, 256), F32),
            pltpu.VMEM((512, 128), F32),
            pltpu.VMEM((16, 512, 256), BF16),
            pltpu.VMEM((512, 384), F32),
            pltpu.VMEM((256, 384), BF16),
            pltpu.VMEM((256, 384), BF16),
            pltpu.VMEM((512, 384), BF16),
            pltpu.VMEM((8, 64, 384), BF16),
            pltpu.VMEM((256, 512), BF16),
            pltpu.VMEM((512, 256), BF16),
            pltpu.VMEM((256, 128), F32),
            dma((4,)),
            dma((2, 5, 4)),
            dma((2, 4, 4)),
            dma((2, 5, 4)),
            dma((2, 4, 4)),
            dma((2, 5, 4)),
            dma((2, 4, 4)),
            dma((4, 5)),
            dma((4, 5)),
            dma((4, 8)),
            dma((4, 8)),
        ],
        compiler_params=pltpu.CompilerParams(
            collective_id=0, has_side_effects=True, vmem_limit_bytes=48 << 20
        ),
    )(
        attn,
        out_proj,
        residual[0],
        norm_gain.reshape(16, 384),
        jnp.swapaxes(expert_ids, 1, 2),
        jnp.swapaxes(gate_weights, 1, 2),
        expert_gate[0],
        expert_up[0],
        expert_down[0],
    )
    return (stream[None], mix[None])


def solution(mesh):
    return jax.shard_map(
        local,
        mesh=mesh,
        in_specs=(
            P("role", "grp", "tp"),
            P("role", "grp", "tp"),
            P("role", "grp", "tp"),
            P("role", "grp", "tp", None, None),
            P("role", "grp", "tp", None, None),
            P("role", "grp"),
            P("tp", "grp"),
            P("role", None, "grp"),
            P(),
            P(),
            P(),
            P("tp", None, ("role", "grp")),
            P("tp", None, ("role", "grp")),
            P("tp", "role", "grp"),
        ),
        out_specs=(P("role", None, "grp"), P("role", None, "grp")),
        check_vma=False,
    )
```

```python
import math

import jax
import jax.numpy as jnp
from jax import lax
from jax.experimental import pallas as pl
from jax.experimental.pallas import tpu as pltpu
from jax.sharding import PartitionSpec as P

MESH = pl.DeviceIdType.MESH
BF16 = jnp.bfloat16
F32 = jnp.float32
D = 6144
SIDE = 4
GROUPS = 16
PLANES = 8
ROWS = 128


def remote(src, dst, send_sem, recv_sem, device):
    return pltpu.make_async_remote_copy(
        src_ref=src,
        dst_ref=dst,
        send_sem=send_sem,
        recv_sem=recv_sem,
        device_id=device,
        device_id_type=MESH,
    )


class Torus:
    def __init__(self, role, x, y, plane):
        self.role, self.plane = role, plane
        self.xs = [lax.rem(x + k, SIDE) * SIDE for k in range(SIDE)]
        self.ys = [lax.rem(y + k, SIDE) for k in range(SIDE)]

    def at(self, half, first, second):
        dx, dy = (first, second) if half == 0 else (second, first)
        return self.xs[dx] + self.ys[dy]

    def device(self, half, first, second):
        return (self.role, self.at(half, first, second), self.plane)


class PlaneGather:
    def __init__(self, torus, blocks, piece, send, recv):
        self.torus, self.blocks, self.piece, self.send, self.recv = torus, blocks, piece, send, recv

    def copy(self, half, first, phase, step):
        piece = self.piece(self.torus.at(half, first, 0), half)
        if phase == 0:
            target = self.torus.device(half, step, 0)
            recv = self.recv.at[half * SIDE + SIDE - step]
        else:
            target = self.torus.device(half, 0, step)
            recv = self.recv.at[2 * SIDE + (first if half == 0 else SIDE - step)]
        return remote(piece, piece, self.send, recv, target)

    def taken(self, ref, which):
        remote(ref, ref, self.send, self.recv.at[which], self.torus.device(0, 1, 0)).wait_recv()

    def start(self):
        for phase in range(2):
            for step in (1, 3, 2):
                for half in (0, 1):
                    self.copy(half, 0, phase, step).start()

    def forward(self):
        for first in (1, 3, 2):
            for half in (0, 1):
                self.taken(self.piece(self.torus.at(half, first, 0), half), half * SIDE + first)
                for step in (1, 3, 2):
                    self.copy(half, first, 1, step).start()

    def row(self, dx, halves):
        self.taken(self.blocks(halves), 2 * SIDE + dx)

    def finish(self):
        ref = self.blocks(30)
        remote(ref, ref, self.send, self.recv.at[0], self.torus.device(0, 1, 0)).wait_send()


class RelayGather:
    def __init__(self, torus, blocks, piece, send, recv):
        self.torus, self.blocks, self.piece, self.send, self.recv = torus, blocks, piece, send, recv

    def first_axis(self, half, step):
        piece = self.piece(self.torus.at(half, 0, 0), half, None)
        recv = self.recv.at[SIDE - step]
        remote(piece, piece, self.send, recv, self.torus.device(half, step, 0)).start()

    def second_axis(self, half, first, step):
        piece = self.piece(self.torus.at(half, first, 0), half, None)
        recv = self.recv.at[SIDE + 2 * first + (SIDE - step) // 2]
        remote(piece, piece, self.send, recv, self.torus.device(half, 0, step)).start()

    def pass_on(self, half, first, side):
        piece = self.piece(self.torus.at(half, first, side), half, side // 2)
        recv = self.recv.at[3 * SIDE + first]
        remote(piece, piece, self.send, recv, self.torus.device(half, 0, SIDE - side)).start()

    def taken(self, which):
        ref = self.blocks(1)
        remote(ref, ref, self.send, self.recv.at[which], self.torus.device(0, 1, 0)).wait_recv()

    def start(self):
        for step in (1, 3, 2):
            for half in (0, 1):
                self.first_axis(half, step)
        for step in (1, 3):
            for half in (0, 1):
                self.second_axis(half, 0, step)

    def turn(self):
        for first in (1, 3, 2):
            self.taken(first)
            for step in (1, 3):
                for half in (0, 1):
                    self.second_axis(half, first, step)

    def relay(self, first):
        for side in (1, 3):
            self.taken(SIDE + 2 * first + side // 2)
            for half in (0, 1):
                self.pass_on(half, first, side)

    def far(self):
        for first in (0, 1, 3, 2):
            self.taken(3 * SIDE + first)

    def finish(self):
        ref = self.blocks(15)
        remote(ref, ref, self.send, self.recv.at[0], self.torus.device(0, 1, 0)).wait_send()


def near_side(i):
    return i + i // 2


def attend(query_ref, key_ref, value_ref, lengths_ref, keys, values, arrive, spread_q, fresh_kv, scores, mixed, out):
    factor = 1.0 / math.sqrt(128)
    spread_q[...] = jnp.zeros_like(spread_q)
    query = query_ref[...].astype(F32)
    fresh_kv[0] = key_ref[...].astype(F32)
    fresh_kv[1] = value_ref[...].astype(F32)
    for head in range(6):
        spread_q[:, head, :] = query[:, head * 128 : head * 128 + 128]
    position = lax.broadcasted_iota(jnp.int32, (8, 256), 1)

    def group(i, carry):
        some = pl.ds(i * 8, 8)
        arrive(0, i)
        for k in range(8):
            s = i * 8 + k
            raw = lax.dot_general(
                spread_q[s].astype(BF16),
                keys[s],
                (((1,), (1,)), ((), ())),
                preferred_element_type=F32,
            )
            scores[s] = jnp.where(position < lengths_ref[0, s], raw * factor, -jnp.inf)
        rows = pl.ds(pl.multiple_of(i * 8, 8), 8)
        fresh_key = fresh_kv[0, rows, :][:, None, :]
        fresh = jnp.sum(spread_q[some] * fresh_key, axis=-1, keepdims=True) * factor
        score = scores[some]
        highest = jnp.maximum(jnp.max(score, axis=-1, keepdims=True), fresh)
        weights = jnp.exp(score - highest)
        own = jnp.exp(fresh - highest)
        denominator = jnp.sum(weights, axis=-1, keepdims=True) + own
        probs = (weights / denominator).astype(BF16)
        own_prob = (own / denominator).astype(BF16).astype(F32)
        fresh_value = fresh_kv[1, rows, :][:, None, :]
        own_part = own_prob * fresh_value
        arrive(1, i)
        for k in range(8):
            s = i * 8 + k
            mixed[s] = jnp.dot(probs[k], values[s], preferred_element_type=F32) + own_part[k]
        return carry

    lax.fori_loop(0, 4, group, 0)
    for head in range(6):
        out[:, head * 128 : head * 128 + 128] = mixed[:, head, :].astype(BF16)


def layer(
    lengths_ref,
    query_hbm,
    new_key_hbm,
    new_value_hbm,
    keys_hbm,
    values_hbm,
    proj_hbm,
    resid_hbm,
    gain_hbm,
    ids_hbm,
    gates_hbm,
    gate_hbm,
    up_hbm,
    down_hbm,
    stream_ref,
    mix_ref,
    query,
    new_key,
    new_value,
    keys,
    values,
    spread_q,
    fresh_kv,
    scores,
    mixed,
    attn_mine,
    attn_all,
    proj,
    resid_ref,
    gain_ref,
    ids_ref,
    gates_ref,
    gate_w,
    up_w,
    down_w,
    heads,
    head_in,
    rows_all,
    gate_acc,
    up_acc,
    square_acc,
    hidden_all,
    down_acc,
    half_out,
    half_in,
    mix_part,
    mix_in,
    pick,
    place_t,
    weight_col,
    load_sem,
    cache_sem,
    attn_send,
    attn_recv,
    rows_send,
    rows_recv,
    hid_send,
    hid_recv,
    sib_send,
    sib_recv,
    swap_send,
    swap_recv,
    z_send,
    z_recv,
):
    role = lax.axis_index("role")
    grp = lax.axis_index("grp")
    plane = lax.axis_index("tp")
    x, y = grp // SIDE, lax.rem(grp, SIDE)
    torus = Torus(role, x, y, plane)
    sibling = (1 - role, grp, plane)

    def along_z(step):
        return (role, grp, lax.rem(plane + step, PLANES))

    barrier = pltpu.get_barrier_semaphore()
    near = [(role, lax.rem(x + k, SIDE) * SIDE + y, plane) for k in (1, 2, 3)]
    near += [(role, x * SIDE + lax.rem(y + k, SIDE), plane) for k in (1, 2, 3)]
    near += [along_z(k) for k in range(1, PLANES)] + [sibling]
    for device in near:
        pl.semaphore_signal(barrier, inc=1, device_id=device, device_id_type=MESH)

    pairs = (
        (query_hbm, query),
        (new_key_hbm, new_key),
        (new_value_hbm, new_value),
        (ids_hbm, ids_ref),
        (gates_hbm, gates_ref),
        (gain_hbm, gain_ref),
        (proj_hbm, proj),
        (resid_hbm, resid_ref),
        (gate_hbm, gate_w),
        (up_hbm, up_w),
        (down_hbm, down_w),
    )
    loads = [pltpu.make_async_copy(src, dst, load_sem.at[i]) for i, (src, dst) in enumerate(pairs)]

    def cache_load(which, i):
        src, dst = ((keys_hbm, keys), (values_hbm, values))[which]
        some = pl.ds(i * 8, 8)
        return pltpu.make_async_copy(src.at[some], dst.at[some], cache_sem.at[which, i])

    for load in loads[:3]:
        load.start()
    for i in range(4):
        cache_load(0, i).start()
        cache_load(1, i).start()
    for load in loads[3:]:
        load.start()
    for load in loads[:3]:
        load.wait()
    attend(
        query,
        new_key,
        new_value,
        lengths_ref,
        keys,
        values,
        lambda which, i: cache_load(which, i).wait(),
        spread_q,
        fresh_kv,
        scores,
        mixed,
        attn_mine,
    )
    attn_all[pl.ds(grp * 32, 32), :] = attn_mine[...]
    pl.semaphore_wait(barrier, len(near))

    attn = PlaneGather(
        torus,
        lambda halves: attn_all.at[pl.ds(0, halves * 16)],
        lambda g, half: attn_all.at[pl.ds(g * 32 + half * 16, 16)],
        attn_send.at[0],
        attn_recv,
    )
    attn.start()

    for load in loads[3:8]:
        load.wait()
    ids = ids_ref[role]
    hit0, hit1 = ids[0:1, :] == plane, ids[1:2, :] == plane
    named = jnp.where(hit0 | hit1, 1.0, 0.0)
    gates = gates_ref[role]
    weight_row = jnp.where(hit0, gates[0:1, :], gates[1:2, :])
    seqs = named.shape[1]
    slots = pick.shape[0]
    earlier = lax.broadcasted_iota(jnp.int32, (seqs, seqs), 0) < lax.broadcasted_iota(
        jnp.int32, (seqs, seqs), 1
    )
    before = jnp.dot(
        jnp.broadcast_to(named, (16, seqs)).astype(BF16),
        jnp.where(earlier, 1.0, 0.0).astype(BF16),
        preferred_element_type=F32,
    )[0:1, :]
    slot = jnp.where(named > 0.5, before, -1.0).astype(jnp.int32)
    chosen = jnp.where(slot == lax.broadcasted_iota(jnp.int32, (slots, seqs), 0), 1.0, 0.0)
    pick[...] = chosen.astype(BF16)

    attn.forward()

    place_t[...] = chosen.T.astype(BF16)
    weight_col[...] = jnp.broadcast_to(
        jnp.sum(chosen * weight_row, axis=1, keepdims=True), weight_col.shape
    )
    gate_acc[...] = jnp.zeros_like(gate_acc)
    up_acc[...] = jnp.zeros_like(up_acc)
    square_acc[...] = jnp.zeros_like(square_acc)
    down_acc[...] = jnp.zeros_like(down_acc)

    mine = pl.ds(plane * 64, 64)

    def part_for(src, dst, s, step):
        to = lax.rem(plane + step, PLANES)
        sems = z_send.at[s], z_recv.at[s]
        return remote(src.at[pl.ds(to * 64, 64)], dst.at[step], *sems, along_z(step))

    def seven(ref, s):
        ref = ref.at[pl.ds(0, 7 * 64)]
        return remote(ref, ref, z_send.at[s], z_recv.at[s], along_z(1))

    def project(dx):
        row = lax.rem(x + dx, SIDE)
        some = pl.ds(row * 128, 128)
        part = jnp.dot(attn_all[some, :], proj[...], preferred_element_type=F32)
        heads[some, :] = part.astype(BF16)
        for k in range(2):
            step = lax.rem(2 * row + k + PLANES - plane, PLANES)

            @pl.when(step != 0)
            def _():
                part_for(heads, head_in, 0, step).start()

    attn.row(0, 3)
    project(0)

    def attn_rest(i, carry):
        dx = jnp.where(i == 2, 2, 2 * i + 1)
        attn.row(dx, 7)
        project(dx)
        return carry

    lax.fori_loop(0, 3, attn_rest, 0)

    def collect(src, dst, s):
        seven(src, s).wait_recv()

        def add(step, carry):
            return carry + dst[step].astype(F32)

        return lax.fori_loop(1, PLANES, add, src[mine, :].astype(F32))

    def spread(ref, s):
        def go(step, carry):
            block = ref.at[mine]
            remote(block, block, z_send.at[s], z_recv.at[s], along_z(step)).start()
            return carry

        lax.fori_loop(1, PLANES, go, 0)
        seven(ref, s).wait_recv()

    summed = collect(heads, head_in, 0)
    stream_ref[mine, :] = (resid_ref[mine, :].astype(F32) + summed).astype(BF16)
    spread(stream_ref, 1)

    def gain_of(g):
        return jnp.concatenate([gain_ref[pl.ds(g * 3 + k, 1), :] for k in range(3)], axis=1)

    scaled = (stream_ref[...].astype(F32) * gain_of(grp)).astype(BF16)
    rows = []
    for k in range(2):
        some = pl.ds(k * ROWS, ROWS)
        rows_all[role, grp, some, :] = jnp.dot(
            pick[some, :], scaled, preferred_element_type=F32
        ).astype(BF16)

        def rows_piece(g, half, part, k=k):
            start = k * ROWS + half * 64 + 32 * (part or 0)
            return rows_all.at[role, g, pl.ds(start, 64 if part is None else 32)]

        def rows_blocks(count, k=k):
            return rows_all.at[role, pl.ds(0, count), pl.ds(k * ROWS, ROWS)]

        rows.append(RelayGather(torus, rows_blocks, rows_piece, rows_send.at[k], rows_recv.at[k]))
        rows[k].start()

    def block_at(dx, dy):
        return lax.rem(x + dx, SIDE) * SIDE + lax.rem(y + dy, SIDE)

    def share(k, group, dx, dy):
        block = rows_all.at[role, block_at(dx, dy), pl.ds(k * ROWS, ROWS)]
        remote(block, block, sib_send.at[0], sib_recv.at[k, group], sibling).start()

    def shared(k, group, count):
        ref = rows_all.at[1 - role, pl.ds(0, count), pl.ds(k * ROWS, ROWS)]
        remote(ref, ref, sib_send.at[0], sib_recv.at[k, group], sibling).wait_recv()

    def expert_in(k, dx, dy):
        g = block_at(dx, dy)
        depth = pl.ds(pl.multiple_of(g * 384, 128), 384)
        block = rows_all[:, g, pl.ds(k * ROWS, ROWS), :].reshape(2 * ROWS, 384)
        gate_acc[k] += jnp.dot(block, gate_w[depth, :], preferred_element_type=F32)
        up_acc[k] += jnp.dot(block, up_w[depth, :], preferred_element_type=F32)
        plain = block.astype(F32) * (1.0 / gain_of(g))
        plain = plain * plain
        square_acc[k] += plain[:, :128] + plain[:, 128:256] + plain[:, 256:]

    def beside(i):
        a = 1 + 2 * lax.rem(i, 2)
        return jnp.where(i < 2, a, 0), jnp.where(i < 2, 0, a)

    def across(i):
        return 1 + 2 * (i // 2), 1 + 2 * lax.rem(i, 2)

    def far(i):
        return (
            jnp.where(i < 3, 2, jnp.where(i < 6, near_side(i - 3), 2)),
            jnp.where(i < 3, near_side(i), 2),
        )

    def each(count, where, one):
        def body(i, carry):
            one(*where(i))
            return carry

        lax.fori_loop(0, count, body, 0)

    def share_all(k, group, count, where):
        each(count, where, lambda dx, dy: share(k, group, dx, dy))

    def enter(k, group, count, where):
        shared(k, group, count)
        each(count, where, lambda dx, dy: expert_in(k, dx, dy))

    hid = []

    def hidden(k):
        mean = jnp.sum(square_acc[k], axis=1, keepdims=True) / D
        rstat = 1.0 / jnp.sqrt(mean + 1e-05)
        act = gate_acc[k] * rstat
        hidden_all[k, grp] = (act / (1.0 + jnp.exp(-act)) * (up_acc[k] * rstat)).astype(BF16)

        def piece(g, half, part):
            start = half * ROWS + 64 * (part or 0)
            return hidden_all.at[k, g, pl.ds(start, ROWS if part is None else 64)]

        hid.append(
            RelayGather(
                torus,
                lambda count: hidden_all.at[k, pl.ds(0, count)],
                piece,
                hid_send.at[k],
                hid_recv.at[k],
            )
        )
        hid[k].start()

    def expert_out(k, dx, dy):
        g = block_at(dx, dy)
        depth = pl.ds(pl.multiple_of(g * 256, 256), 256)
        down_acc[k] += jnp.dot(hidden_all[k, g], down_w[depth, :], preferred_element_type=F32)

    def swap(k):
        some = pl.ds(k * ROWS, ROWS)
        sems = swap_send.at[k], swap_recv.at[k]
        return remote(half_out.at[some], half_in.at[some], *sems, sibling)

    def leave(k, count, where):
        each(count, where, lambda dx, dy: expert_out(k, dx, dy))

    def leave_near(k):
        expert_out(k, 0, 0)
        leave(k, 4, beside)
        leave(k, 4, across)

    def leave_far(k):
        hid[k].far()
        leave(k, 7, far)
        theirs = down_acc[k, pl.ds((1 - role) * ROWS, ROWS), :]
        half_out[pl.ds(k * ROWS, ROWS), :] = theirs.astype(BF16)
        swap(k).start()

    for k in range(2):
        share(k, 0, 0, 0)
    for k in range(2):
        rows[k].turn()
    loads[8].wait()
    loads[9].wait()
    for k in range(2):
        shared(k, 0, 1)
        expert_in(k, 0, 0)
    for k in range(2):
        rows[k].relay(0)
        share_all(k, 1, 4, beside)
    for k in range(2):
        rows[k].relay(1)
        share(k, 2, 1, 1)
    enter(0, 1, 4, beside)
    for k in range(2):
        rows[k].relay(3)
        share(k, 2, 1, 3)
        share(k, 2, 3, 1)
        share(k, 2, 3, 3)
    enter(1, 1, 4, beside)
    for k in range(2):
        rows[k].relay(2)
    enter(0, 2, 4, across)
    rows[0].far()
    share_all(0, 3, 7, far)
    enter(1, 2, 4, across)
    enter(0, 3, 7, far)
    hidden(0)
    rows[1].far()
    share_all(1, 3, 7, far)
    loads[10].wait()
    enter(1, 3, 7, far)
    hidden(1)
    for k in range(2):
        hid[k].turn()
    for first in (0, 1, 3, 2):
        hid[0].relay(first)
    leave_near(0)
    for first in (0, 1):
        hid[1].relay(first)
    leave_far(0)
    for first in (3, 2):
        hid[1].relay(first)
    leave_near(1)
    leave_far(1)

    weighted = []
    for k in range(2):
        swap(k).wait_recv()
        some = pl.ds(k * ROWS, ROWS)
        whole = down_acc[k, pl.ds(role * ROWS, ROWS), :] + half_in[some, :].astype(F32)
        weighted.append((whole * weight_col[some, 0:1]).astype(BF16))
    weighted = jnp.concatenate(weighted, axis=0)
    mix_part[...] = jnp.dot(place_t[...], weighted, preferred_element_type=F32).astype(BF16)

    def mix_go(step, carry):
        part_for(mix_part, mix_in, 2, step).start()
        return carry

    lax.fori_loop(1, PLANES, mix_go, 0)
    mix_ref[mine, :] = collect(mix_part, mix_in, 2).astype(BF16)
    spread(mix_ref, 3)

    attn.finish()
    for k in range(2):
        rows[k].finish()
        hid[k].finish()
        swap(k).wait_send()

    for i, ref in enumerate((heads, stream_ref, mix_part, mix_ref)):
        seven(ref, i).wait_send()
    everything = rows_all.at[role]
    remote(everything, everything, sib_send.at[0], sib_recv.at[0, 0], sibling).wait_send()


def local(
    queries,
    new_keys,
    new_values,
    cache_keys,
    cache_values,
    lengths,
    out_proj,
    residual,
    norm_gain,
    expert_ids,
    gate_weights,
    expert_gate,
    expert_up,
    expert_down,
):
    vmem = pl.BlockSpec(memory_space=pltpu.VMEM)
    hbm = pl.BlockSpec(memory_space=pl.ANY)
    dma = pltpu.SemaphoreType.DMA
    stream, mix = pl.pallas_call(
        layer,
        out_shape=(
            jax.ShapeDtypeStruct((512, 384), BF16),
            jax.ShapeDtypeStruct((512, 384), BF16),
        ),
        in_specs=[pl.BlockSpec(memory_space=pltpu.SMEM)] + [hbm] * 13,
        out_specs=(vmem, vmem),
        scratch_shapes=[
            pltpu.VMEM((32, 768), BF16),
            pltpu.VMEM((32, 128), BF16),
            pltpu.VMEM((32, 128), BF16),
            pltpu.VMEM((32, 256, 128), BF16),
            pltpu.VMEM((32, 256, 128), BF16),
            pltpu.VMEM((32, 8, 128), F32),
            pltpu.VMEM((2, 32, 128), F32),
            pltpu.VMEM((32, 8, 256), F32),
            pltpu.VMEM((32, 8, 128), F32),
            pltpu.VMEM((32, 768), BF16),
            pltpu.VMEM((512, 768), BF16),
            pltpu.VMEM((768, 384), BF16),
            pltpu.VMEM((512, 384), BF16),
            pltpu.VMEM((48, 128), F32),
            pltpu.VMEM((2, 2, 512), jnp.int32),
            pltpu.VMEM((2, 2, 512), F32),
            pltpu.VMEM((6144, 256), BF16),
            pltpu.VMEM((6144, 256), BF16),
            pltpu.VMEM((4096, 384), BF16),
            pltpu.VMEM((512, 384), BF16),
            pltpu.VMEM((8, 64, 384), BF16),
            pltpu.VMEM((2, 16, 256, 384), BF16),
            pltpu.VMEM((2, 256, 256), F32),
            pltpu.VMEM((2, 256, 256), F32),
            pltpu.VMEM((2, 256, 128), F32),
            pltpu.VMEM((2, 16, 256, 256), BF16),
            pltpu.VMEM((2, 256, 384), F32),
            pltpu.VMEM((256, 384), BF16),
            pltpu.VMEM((256, 384), BF16),
            pltpu.VMEM((512, 384), BF16),
            pltpu.VMEM((8, 64, 384), BF16),
            pltpu.VMEM((256, 512), BF16),
            pltpu.VMEM((512, 256), BF16),
            pltpu.VMEM((256, 128), F32),
            dma((11,)),
            dma((2, 4)),
            dma((1,)),
            dma((12,)),
            dma((2,)),
            dma((2, 16)),
            dma((2,)),
            dma((2, 16)),
            dma((1,)),
            dma((2, 4)),
            dma((2,)),
            dma((2,)),
            dma((4,)),
            dma((4,)),
        ],
        compiler_params=pltpu.CompilerParams(
            collective_id=0, has_side_effects=True, vmem_limit_bytes=56 << 20
        ),
    )(
        lengths,
        queries[0],
        new_keys[0],
        new_values[0],
        cache_keys.reshape(32, 256, 128),
        cache_values.reshape(32, 256, 128),
        out_proj,
        residual[0],
        norm_gain.reshape(48, 128),
        jnp.swapaxes(expert_ids, 1, 2),
        jnp.swapaxes(gate_weights, 1, 2),
        expert_gate[0],
        expert_up[0],
        expert_down[0],
    )
    return (stream[None], mix[None])


def solution(mesh):
    return jax.shard_map(
        local,
        mesh=mesh,
        in_specs=(
            P("role", "grp", "tp"),
            P("role", "grp", "tp"),
            P("role", "grp", "tp"),
            P("role", "grp", "tp", None, None),
            P("role", "grp", "tp", None, None),
            P("role", "grp"),
            P("tp", "grp"),
            P("role", None, "grp"),
            P(),
            P(),
            P(),
            P("tp", None, ("role", "grp")),
            P("tp", None, ("role", "grp")),
            P("tp", "role", "grp"),
        ),
        out_specs=(P("role", None, "grp"), P("role", None, "grp")),
        check_vma=False,
    )
```

```python
import math

import jax
import jax.numpy as jnp
from jax import lax
from jax.experimental import pallas as pl
from jax.experimental.pallas import tpu as pltpu
from jax.sharding import PartitionSpec as P

MESH = pl.DeviceIdType.MESH
BF16 = jnp.bfloat16
F32 = jnp.float32
D = 6144
SIDE = 4
GROUPS = 16
PLANES = 8
FARTHEST_FIRST = (4, 3, 5, 2, 6, 1, 7)


def remote(src, dst, send_sem, recv_sem, device):
    return pltpu.make_async_remote_copy(
        src_ref=src,
        dst_ref=dst,
        send_sem=send_sem,
        recv_sem=recv_sem,
        device_id=device,
        device_id_type=MESH,
    )


class Torus:
    def __init__(self, role, x, y, plane):
        self.role, self.plane = role, plane
        self.xs = [lax.rem(x + k, SIDE) * SIDE for k in range(SIDE)]
        self.ys = [lax.rem(y + k, SIDE) for k in range(SIDE)]

    def at(self, half, first, second):
        dx, dy = (first, second) if half == 0 else (second, first)
        return self.xs[dx] + self.ys[dy]

    def device(self, half, first, second):
        return (self.role, self.at(half, first, second), self.plane)


class PlaneGather:
    def __init__(self, torus, blocks, piece, send, recv):
        self.torus, self.blocks, self.piece, self.send, self.recv = torus, blocks, piece, send, recv

    def copy(self, half, first, phase, step):
        piece = self.piece(self.torus.at(half, first, 0), half)
        if phase == 0:
            target = self.torus.device(half, step, 0)
            recv = self.recv.at[half * SIDE + SIDE - step]
        else:
            target = self.torus.device(half, 0, step)
            recv = self.recv.at[2 * SIDE + (first if half == 0 else SIDE - step)]
        return remote(piece, piece, self.send, recv, target)

    def taken(self, ref, which):
        remote(ref, ref, self.send, self.recv.at[which], self.torus.device(0, 1, 0)).wait_recv()

    def start(self):
        for phase in range(2):
            for step in (1, 3, 2):
                for half in (0, 1):
                    self.copy(half, 0, phase, step).start()

    def forward(self):
        for first in (1, 3, 2):
            for half in (0, 1):
                self.taken(self.piece(self.torus.at(half, first, 0), half), half * SIDE + first)
                for step in (1, 3, 2):
                    self.copy(half, first, 1, step).start()

    def row(self, dx, halves):
        self.taken(self.blocks(halves), 2 * SIDE + dx)

    def finish(self):
        ref = self.blocks(30)
        remote(ref, ref, self.send, self.recv.at[0], self.torus.device(0, 1, 0)).wait_send()


class RelayGather:
    def __init__(self, torus, blocks, piece, send, recv):
        self.torus, self.blocks, self.piece, self.send, self.recv = torus, blocks, piece, send, recv

    def first_axis(self, half, step):
        piece = self.piece(self.torus.at(half, 0, 0), half, None)
        recv = self.recv.at[SIDE - step]
        remote(piece, piece, self.send, recv, self.torus.device(half, step, 0)).start()

    def second_axis(self, half, first, step):
        piece = self.piece(self.torus.at(half, first, 0), half, None)
        recv = self.recv.at[SIDE + 2 * first + (SIDE - step) // 2]
        remote(piece, piece, self.send, recv, self.torus.device(half, 0, step)).start()

    def pass_on(self, half, first, side):
        piece = self.piece(self.torus.at(half, first, side), half, side // 2)
        recv = self.recv.at[3 * SIDE + first]
        remote(piece, piece, self.send, recv, self.torus.device(half, 0, SIDE - side)).start()

    def taken(self, which):
        ref = self.blocks(1)
        remote(ref, ref, self.send, self.recv.at[which], self.torus.device(0, 1, 0)).wait_recv()

    def start(self):
        for step in (2, 1, 3):
            for half in (0, 1):
                self.first_axis(half, step)
        for step in (1, 3):
            for half in (0, 1):
                self.second_axis(half, 0, step)

    def turn(self):
        for first in (1, 3, 2):
            self.taken(first)
            for step in (1, 3):
                for half in (0, 1):
                    self.second_axis(half, first, step)

    def relay(self, first):
        for side in (1, 3):
            self.taken(SIDE + 2 * first + side // 2)
            for half in (0, 1):
                self.pass_on(half, first, side)

    def far(self, first):
        self.taken(3 * SIDE + first)

    def finish(self):
        ref = self.blocks(15)
        remote(ref, ref, self.send, self.recv.at[0], self.torus.device(0, 1, 0)).wait_send()


def near_side(i):
    return i + i // 2


def attend(query_ref, key_ref, value_ref, lengths_ref, keys, values, arrive, spread_q, fresh_kv, scores, mixed, out):
    factor = 1.0 / math.sqrt(128)
    spread_q[...] = jnp.zeros_like(spread_q)
    query = query_ref[...].astype(F32)
    fresh_kv[0] = key_ref[...].astype(F32)
    fresh_kv[1] = value_ref[...].astype(F32)
    for head in range(6):
        spread_q[:, head, :] = query[:, head * 128 : head * 128 + 128]
    position = lax.broadcasted_iota(jnp.int32, (8, 256), 1)

    def group(i, carry):
        some = pl.ds(i * 8, 8)
        arrive(0, i)
        for k in range(8):
            s = i * 8 + k
            raw = lax.dot_general(
                spread_q[s].astype(BF16),
                keys[s],
                (((1,), (1,)), ((), ())),
                preferred_element_type=F32,
            )
            scores[s] = jnp.where(position < lengths_ref[0, s], raw * factor, -jnp.inf)
        rows = pl.ds(pl.multiple_of(i * 8, 8), 8)
        fresh_key = fresh_kv[0, rows, :][:, None, :]
        fresh = jnp.sum(spread_q[some] * fresh_key, axis=-1, keepdims=True) * factor
        score = scores[some]
        highest = jnp.maximum(jnp.max(score, axis=-1, keepdims=True), fresh)
        weights = jnp.exp(score - highest)
        own = jnp.exp(fresh - highest)
        denominator = jnp.sum(weights, axis=-1, keepdims=True) + own
        probs = (weights / denominator).astype(BF16)
        own_prob = (own / denominator).astype(BF16).astype(F32)
        fresh_value = fresh_kv[1, rows, :][:, None, :]
        own_part = own_prob * fresh_value
        arrive(1, i)
        for k in range(8):
            s = i * 8 + k
            mixed[s] = jnp.dot(probs[k], values[s], preferred_element_type=F32) + own_part[k]
        return carry

    lax.fori_loop(0, 4, group, 0)
    for head in range(6):
        out[:, head * 128 : head * 128 + 128] = mixed[:, head, :].astype(BF16)


def layer(
    lengths_hbm,
    query_hbm,
    new_key_hbm,
    new_value_hbm,
    keys_hbm,
    values_hbm,
    proj_hbm,
    resid_hbm,
    gain_hbm,
    ids_hbm,
    gates_hbm,
    gate_hbm,
    up_hbm,
    down_hbm,
    stream_ref,
    mix_ref,
    lengths_ref,
    query,
    new_key,
    new_value,
    keys,
    values,
    spread_q,
    fresh_kv,
    scores,
    mixed,
    attn_mine,
    attn_all,
    proj,
    resid_ref,
    gain_ref,
    ids_ref,
    gates_ref,
    gate_w,
    up_w,
    down_w,
    heads,
    head_in,
    rows_all,
    gate_acc,
    up_acc,
    square_acc,
    hidden_all,
    down_acc,
    half_out,
    half_in,
    mix_part,
    mix_in,
    pick,
    place_t,
    weight_col,
    load_sem,
    cache_sem,
    attn_send,
    attn_recv,
    rows_send,
    rows_recv,
    hid_send,
    hid_recv,
    sib_send,
    sib_recv,
    swap_send,
    swap_recv,
    z_send,
    z_recv,
):
    role = lax.axis_index("role")
    grp = lax.axis_index("grp")
    plane = lax.axis_index("tp")
    x, y = grp // SIDE, lax.rem(grp, SIDE)
    torus = Torus(role, x, y, plane)
    sibling = (1 - role, grp, plane)

    def along_z(step):
        return (role, grp, lax.rem(plane + step, PLANES))

    barrier = pltpu.get_barrier_semaphore()
    near = [along_z(k) for k in FARTHEST_FIRST]
    near += [(role, lax.rem(x + k, SIDE) * SIDE + y, plane) for k in (2, 1, 3)]
    near += [(role, x * SIDE + lax.rem(y + k, SIDE), plane) for k in (2, 1, 3)]
    near += [sibling]
    for device in near:
        pl.semaphore_signal(barrier, inc=1, device_id=device, device_id_type=MESH)

    pairs = (
        (lengths_hbm, lengths_ref),
        (query_hbm, query),
        (new_key_hbm, new_key),
        (new_value_hbm, new_value),
        (ids_hbm, ids_ref),
        (gates_hbm, gates_ref),
        (gain_hbm, gain_ref),
        (proj_hbm, proj),
        (resid_hbm, resid_ref),
        (gate_hbm, gate_w),
        (up_hbm, up_w),
        (down_hbm, down_w),
    )
    loads = [pltpu.make_async_copy(src, dst, load_sem.at[i]) for i, (src, dst) in enumerate(pairs)]

    def cache_load(which, i):
        src, dst = ((keys_hbm, keys), (values_hbm, values))[which]
        some = pl.ds(i * 8, 8)
        return pltpu.make_async_copy(src.at[some], dst.at[some], cache_sem.at[which, i])

    for load in loads[:4]:
        load.start()
    for i in range(4):
        cache_load(0, i).start()
        cache_load(1, i).start()
    for load in loads[4:]:
        load.start()
    for load in loads[:4]:
        load.wait()
    attend(
        query,
        new_key,
        new_value,
        lengths_ref,
        keys,
        values,
        lambda which, i: cache_load(which, i).wait(),
        spread_q,
        fresh_kv,
        scores,
        mixed,
        attn_mine,
    )
    attn_all[pl.ds(grp * 32, 32), :] = attn_mine[...]
    pl.semaphore_wait(barrier, len(near))

    attn = PlaneGather(
        torus,
        lambda halves: attn_all.at[pl.ds(0, halves * 16)],
        lambda g, half: attn_all.at[pl.ds(g * 32 + half * 16, 16)],
        attn_send.at[0],
        attn_recv,
    )
    attn.start()

    for load in loads[4:9]:
        load.wait()
    ids = ids_ref[role]
    hit0, hit1 = ids[0:1, :] == plane, ids[1:2, :] == plane
    named = jnp.where(hit0 | hit1, 1.0, 0.0)
    gates = gates_ref[role]
    weight_row = jnp.where(hit0, gates[0:1, :], gates[1:2, :])
    seqs = named.shape[1]
    slots = pick.shape[0]
    earlier = lax.broadcasted_iota(jnp.int32, (seqs, seqs), 0) < lax.broadcasted_iota(
        jnp.int32, (seqs, seqs), 1
    )
    before = jnp.dot(
        jnp.broadcast_to(named, (16, seqs)).astype(BF16),
        jnp.where(earlier, 1.0, 0.0).astype(BF16),
        preferred_element_type=F32,
    )[0:1, :]
    slot = jnp.where(named > 0.5, before, -1.0).astype(jnp.int32)
    chosen = jnp.where(slot == lax.broadcasted_iota(jnp.int32, (slots, seqs), 0), 1.0, 0.0)
    pick[...] = chosen.astype(BF16)

    attn.forward()

    place_t[...] = chosen.T.astype(BF16)
    weight_col[...] = jnp.broadcast_to(
        jnp.sum(chosen * weight_row, axis=1, keepdims=True), weight_col.shape
    )
    gate_acc[...] = jnp.zeros_like(gate_acc)
    up_acc[...] = jnp.zeros_like(up_acc)
    square_acc[...] = jnp.zeros_like(square_acc)
    down_acc[...] = jnp.zeros_like(down_acc)

    mine = pl.ds(plane * 64, 64)

    def part_for(src, dst, s, step):
        to = lax.rem(plane + step, PLANES)
        sems = z_send.at[s], z_recv.at[s]
        return remote(src.at[pl.ds(to * 64, 64)], dst.at[step], *sems, along_z(step))

    def seven(ref, s):
        ref = ref.at[pl.ds(0, 7 * 64)]
        return remote(ref, ref, z_send.at[s], z_recv.at[s], along_z(1))

    def project(dx):
        row = lax.rem(x + dx, SIDE)
        some = pl.ds(row * 128, 128)
        part = jnp.dot(attn_all[some, :], proj[...], preferred_element_type=F32)
        heads[some, :] = part.astype(BF16)
        for k in range(2):
            step = lax.rem(2 * row + k + PLANES - plane, PLANES)

            @pl.when(step != 0)
            def _():
                part_for(heads, head_in, 0, step).start()

    attn.row(0, 3)
    project(0)

    def attn_rest(i, carry):
        dx = jnp.where(i == 2, 2, 2 * i + 1)
        attn.row(dx, 7)
        project(dx)
        return carry

    lax.fori_loop(0, 3, attn_rest, 0)

    def collect(src, dst, s):
        seven(src, s).wait_recv()

        def add(step, carry):
            return carry + dst[step].astype(F32)

        return lax.fori_loop(1, PLANES, add, src[mine, :].astype(F32))

    def spread(ref, s):
        block = ref.at[mine]
        for step in FARTHEST_FIRST:
            remote(block, block, z_send.at[s], z_recv.at[s], along_z(step)).start()
        seven(ref, s).wait_recv()

    summed = collect(heads, head_in, 0)
    stream_ref[mine, :] = (resid_ref[mine, :].astype(F32) + summed).astype(BF16)
    spread(stream_ref, 1)

    def gain_of(g):
        return jnp.concatenate([gain_ref[pl.ds(g * 3 + k, 1), :] for k in range(3)], axis=1)

    scaled = (stream_ref[...].astype(F32) * gain_of(grp)).astype(BF16)
    rows_all[role, grp] = jnp.dot(pick[...], scaled, preferred_element_type=F32).astype(BF16)
    rows = RelayGather(
        torus,
        lambda count: rows_all.at[role, pl.ds(0, count)],
        lambda g, half, part: rows_all.at[
            role, g, pl.ds(half * 128 + 64 * (part or 0), 128 if part is None else 64)
        ],
        rows_send.at[0],
        rows_recv,
    )
    rows.start()

    def block_at(dx, dy):
        return lax.rem(x + dx, SIDE) * SIDE + lax.rem(y + dy, SIDE)

    def share(group, dx, dy):
        block = rows_all.at[role, block_at(dx, dy)]
        remote(block, block, sib_send.at[0], sib_recv.at[group], sibling).start()

    def shared(group, count):
        ref = rows_all.at[1 - role, pl.ds(0, count)]
        remote(ref, ref, sib_send.at[0], sib_recv.at[group], sibling).wait_recv()

    def expert_in(dx, dy):
        g = block_at(dx, dy)
        depth = pl.ds(pl.multiple_of(g * 384, 128), 384)
        block = rows_all[:, g].reshape(512, 384)
        gate_acc[...] += jnp.dot(block, gate_w[depth, :], preferred_element_type=F32)
        up_acc[...] += jnp.dot(block, up_w[depth, :], preferred_element_type=F32)
        plain = block.astype(F32) * (1.0 / gain_of(g))
        plain = plain * plain
        square_acc[...] += plain[:, :128] + plain[:, 128:256] + plain[:, 256:]

    def beside(i):
        a = 1 + 2 * lax.rem(i, 2)
        return jnp.where(i < 2, a, 0), jnp.where(i < 2, 0, a)

    def across(i):
        return 1 + 2 * (i // 2), 1 + 2 * lax.rem(i, 2)

    def far(i):
        return (
            jnp.where(i < 3, 2, jnp.where(i < 6, near_side(i - 3), 2)),
            jnp.where(i < 3, near_side(i), 2),
        )

    def each(count, where, one):
        def body(i, carry):
            one(*where(i))
            return carry

        lax.fori_loop(0, count, body, 0)

    def share_all(group, count, where):
        each(count, where, lambda dx, dy: share(group, dx, dy))

    def enter(group, count, where):
        shared(group, count)
        each(count, where, expert_in)

    share(0, 0, 0)
    rows.turn()
    loads[9].wait()
    loads[10].wait()
    shared(0, 1)
    expert_in(0, 0)
    def far_pair(i, first):
        shared(3 + i, 2)
        expert_in(first, 2)
        expert_in(2, first)

    rows.relay(0)
    share_all(1, 4, beside)
    enter(1, 4, beside)
    rows.relay(1)
    share(2, 1, 1)
    rows.relay(3)
    share(2, 1, 3)
    share(2, 3, 1)
    share(2, 3, 3)
    rows.relay(2)
    for i, first in enumerate((0, 1, 3, 2)):
        rows.far(first)
        if first == 2:
            share(3 + i, 2, 2)
        else:
            share(3 + i, first, 2)
            share(3 + i, 2, first)
        if i == 0:
            enter(2, 4, across)
        else:
            far_pair(i - 1, (0, 1, 3)[i - 1])
    shared(6, 1)
    expert_in(2, 2)

    hid = RelayGather(
        torus,
        lambda count: hidden_all.at[pl.ds(0, count)],
        lambda g, half, part: hidden_all.at[
            g, pl.ds(half * 256 + 128 * (part or 0), 256 if part is None else 128)
        ],
        hid_send.at[0],
        hid_recv,
    )
    mean = jnp.sum(square_acc[...], axis=1, keepdims=True) / D
    rstat = 1.0 / jnp.sqrt(mean + 1e-05)
    act = gate_acc[...] * rstat
    hidden_all[grp] = (act / (1.0 + jnp.exp(-act)) * (up_acc[...] * rstat)).astype(BF16)
    hid.start()

    def expert_out(dx, dy):
        g = block_at(dx, dy)
        depth = pl.ds(pl.multiple_of(g * 256, 256), 256)
        down_acc[...] += jnp.dot(hidden_all[g], down_w[depth, :], preferred_element_type=F32)

    hid.turn()
    loads[11].wait()
    expert_out(0, 0)
    hid.relay(0)
    each(4, beside, expert_out)
    for first in (1, 3, 2):
        hid.relay(first)
    each(4, across, expert_out)
    hid.far(0)
    expert_out(0, 2)
    expert_out(2, 0)
    for first in (1, 3):
        hid.far(first)
        expert_out(first, 2)
        expert_out(2, first)
    hid.far(2)
    expert_out(2, 2)
    half_out[...] = down_acc[pl.ds((1 - role) * 256, 256), :].astype(BF16)
    swap = remote(half_out, half_in, swap_send.at[0], swap_recv.at[0], sibling)
    swap.start()

    swap.wait_recv()
    whole = down_acc[pl.ds(role * 256, 256), :] + half_in[...].astype(F32)
    weighted = (whole * weight_col[:, 0:1]).astype(BF16)
    mix_part[...] = jnp.dot(place_t[...], weighted, preferred_element_type=F32).astype(BF16)

    for step in FARTHEST_FIRST:
        part_for(mix_part, mix_in, 2, step).start()
    attn.finish()
    rows.finish()
    hid.finish()
    for i, ref in ((0, heads), (1, stream_ref)):
        seven(ref, i).wait_send()
    everything = rows_all.at[role]
    remote(everything, everything, sib_send.at[0], sib_recv.at[0], sibling).wait_send()
    mix_ref[mine, :] = collect(mix_part, mix_in, 2).astype(BF16)
    spread(mix_ref, 3)
    swap.wait_send()
    for i, ref in ((2, mix_part), (3, mix_ref)):
        seven(ref, i).wait_send()


def hand_over(stream_ref, mix_ref, stream_out, mix_out):
    stream_out[0] = stream_ref[...]
    mix_out[0] = mix_ref[...]


def local(
    queries,
    new_keys,
    new_values,
    cache_keys,
    cache_values,
    lengths,
    out_proj,
    residual,
    norm_gain,
    expert_ids,
    gate_weights,
    expert_gate,
    expert_up,
    expert_down,
):
    vmem = pl.BlockSpec(memory_space=pltpu.VMEM)
    hbm = pl.BlockSpec(memory_space=pl.ANY)
    dma = pltpu.SemaphoreType.DMA
    stream, mix = pl.pallas_call(
        layer,
        out_shape=(
            jax.ShapeDtypeStruct((512, 384), BF16),
            jax.ShapeDtypeStruct((512, 384), BF16),
        ),
        in_specs=[hbm] * 14,
        out_specs=(vmem, vmem),
        scratch_shapes=[
            pltpu.SMEM((1, 32), jnp.int32),
            pltpu.VMEM((32, 768), BF16),
            pltpu.VMEM((32, 128), BF16),
            pltpu.VMEM((32, 128), BF16),
            pltpu.VMEM((32, 256, 128), BF16),
            pltpu.VMEM((32, 256, 128), BF16),
            pltpu.VMEM((32, 8, 128), F32),
            pltpu.VMEM((2, 32, 128), F32),
            pltpu.VMEM((32, 8, 256), F32),
            pltpu.VMEM((32, 8, 128), F32),
            pltpu.VMEM((32, 768), BF16),
            pltpu.VMEM((512, 768), BF16),
            pltpu.VMEM((768, 384), BF16),
            pltpu.VMEM((512, 384), BF16),
            pltpu.VMEM((48, 128), F32),
            pltpu.VMEM((2, 2, 512), jnp.int32),
            pltpu.VMEM((2, 2, 512), F32),
            pltpu.VMEM((6144, 256), BF16),
            pltpu.VMEM((6144, 256), BF16),
            pltpu.VMEM((4096, 384), BF16),
            pltpu.VMEM((512, 384), BF16),
            pltpu.VMEM((8, 64, 384), BF16),
            pltpu.VMEM((2, 16, 256, 384), BF16),
            pltpu.VMEM((512, 256), F32),
            pltpu.VMEM((512, 256), F32),
            pltpu.VMEM((512, 128), F32),
            pltpu.VMEM((16, 512, 256), BF16),
            pltpu.VMEM((512, 384), F32),
            pltpu.VMEM((256, 384), BF16),
            pltpu.VMEM((256, 384), BF16),
            pltpu.VMEM((512, 384), BF16),
            pltpu.VMEM((8, 64, 384), BF16),
            pltpu.VMEM((256, 512), BF16),
            pltpu.VMEM((512, 256), BF16),
            pltpu.VMEM((256, 128), F32),
            dma((12,)),
            dma((2, 4)),
            dma((1,)),
            dma((12,)),
            dma((1,)),
            dma((16,)),
            dma((1,)),
            dma((16,)),
            dma((1,)),
            dma((7,)),
            dma((1,)),
            dma((1,)),
            dma((4,)),
            dma((4,)),
        ],
        compiler_params=pltpu.CompilerParams(
            collective_id=0, has_side_effects=True, vmem_limit_bytes=56 << 20
        ),
    )(
        lengths,
        queries[0],
        new_keys[0],
        new_values[0],
        cache_keys.reshape(32, 256, 128),
        cache_values.reshape(32, 256, 128),
        out_proj,
        residual[0],
        norm_gain.reshape(48, 128),
        jnp.swapaxes(expert_ids, 1, 2),
        jnp.swapaxes(gate_weights, 1, 2),
        expert_gate[0],
        expert_up[0],
        expert_down[0],
    )
    return pl.pallas_call(
        hand_over,
        out_shape=(jax.ShapeDtypeStruct((1, 512, 384), BF16),) * 2,
        in_specs=[vmem, vmem],
        out_specs=(vmem, vmem),
    )(stream, mix)


def solution(mesh):
    return jax.shard_map(
        local,
        mesh=mesh,
        in_specs=(
            P("role", "grp", "tp"),
            P("role", "grp", "tp"),
            P("role", "grp", "tp"),
            P("role", "grp", "tp", None, None),
            P("role", "grp", "tp", None, None),
            P("role", "grp"),
            P("tp", "grp"),
            P("role", None, "grp"),
            P(),
            P(),
            P(),
            P("tp", None, ("role", "grp")),
            P("tp", None, ("role", "grp")),
            P("tp", "role", "grp"),
        ),
        out_specs=(P("role", None, "grp"), P("role", None, "grp")),
        check_vma=False,
    )
```

```python
import math

import jax
import jax.numpy as jnp
from jax import lax
from jax.experimental import pallas as pl
from jax.experimental.pallas import tpu as pltpu
from jax.sharding import PartitionSpec as P

MESH = pl.DeviceIdType.MESH
BF16 = jnp.bfloat16
F32 = jnp.float32
D = 6144
SIDE = 4
GROUPS = 16
PLANES = 8
FARTHEST_FIRST = (4, 3, 5, 2, 6, 1, 7)


def remote(src, dst, send_sem, recv_sem, device):
    return pltpu.make_async_remote_copy(
        src_ref=src,
        dst_ref=dst,
        send_sem=send_sem,
        recv_sem=recv_sem,
        device_id=device,
        device_id_type=MESH,
    )


class Torus:
    def __init__(self, role, x, y, plane):
        self.role, self.plane = role, plane
        self.xs = [lax.rem(x + k, SIDE) * SIDE for k in range(SIDE)]
        self.ys = [lax.rem(y + k, SIDE) for k in range(SIDE)]

    def at(self, half, first, second):
        dx, dy = (first, second) if half == 0 else (second, first)
        return self.xs[dx] + self.ys[dy]

    def device(self, half, first, second):
        return (self.role, self.at(half, first, second), self.plane)


class PlaneGather:
    def __init__(self, torus, blocks, piece, send, recv):
        self.torus, self.blocks, self.piece, self.send, self.recv = torus, blocks, piece, send, recv

    def copy(self, half, first, phase, step):
        piece = self.piece(self.torus.at(half, first, 0), half)
        if phase == 0:
            target = self.torus.device(half, step, 0)
            recv = self.recv.at[half * SIDE + SIDE - step]
        else:
            target = self.torus.device(half, 0, step)
            recv = self.recv.at[2 * SIDE + (first if half == 0 else SIDE - step)]
        return remote(piece, piece, self.send, recv, target)

    def taken(self, ref, which):
        remote(ref, ref, self.send, self.recv.at[which], self.torus.device(0, 1, 0)).wait_recv()

    def start(self):
        for phase in range(2):
            for step in (2, 1, 3):
                for half in (0, 1):
                    self.copy(half, 0, phase, step).start()

    def forward(self):
        for first in (1, 3, 2):
            for half in (0, 1):
                self.taken(self.piece(self.torus.at(half, first, 0), half), half * SIDE + first)
                for step in (2, 1, 3):
                    self.copy(half, first, 1, step).start()

    def row(self, dx, halves):
        self.taken(self.blocks(halves), 2 * SIDE + dx)

    def finish(self):
        ref = self.blocks(30)
        remote(ref, ref, self.send, self.recv.at[0], self.torus.device(0, 1, 0)).wait_send()


class RelayGather:
    def __init__(self, torus, blocks, piece, send, recv):
        self.torus, self.blocks, self.piece, self.send, self.recv = torus, blocks, piece, send, recv

    def first_axis(self, half, step):
        piece = self.piece(self.torus.at(half, 0, 0), half, None)
        recv = self.recv.at[SIDE - step]
        remote(piece, piece, self.send, recv, self.torus.device(half, step, 0)).start()

    def second_axis(self, half, first, step):
        piece = self.piece(self.torus.at(half, first, 0), half, None)
        recv = self.recv.at[SIDE + 2 * first + (SIDE - step) // 2]
        remote(piece, piece, self.send, recv, self.torus.device(half, 0, step)).start()

    def pass_first(self, half, side):
        piece = self.piece(self.torus.at(half, side, 0), half, side // 2)
        target = self.torus.device(half, SIDE - side, 0)
        remote(piece, piece, self.send, self.recv.at[2], target).start()

    def pass_on(self, half, first, side):
        piece = self.piece(self.torus.at(half, first, side), half, side // 2)
        recv = self.recv.at[3 * SIDE + first]
        remote(piece, piece, self.send, recv, self.torus.device(half, 0, SIDE - side)).start()

    def taken(self, which):
        ref = self.blocks(1)
        remote(ref, ref, self.send, self.recv.at[which], self.torus.device(0, 1, 0)).wait_recv()

    def start(self):
        for step in (1, 3):
            for half in (0, 1):
                self.first_axis(half, step)
        for step in (1, 3):
            for half in (0, 1):
                self.second_axis(half, 0, step)

    def turn(self):
        for first in (1, 3, 2):
            self.taken(first)
            for half in (0, 1) if first != 2 else ():
                self.pass_first(half, first)
            for step in (1, 3):
                for half in (0, 1):
                    self.second_axis(half, first, step)

    def relay(self, first):
        for side in (1, 3):
            self.taken(SIDE + 2 * first + side // 2)
            for half in (0, 1):
                self.pass_on(half, first, side)

    def far(self, first):
        self.taken(3 * SIDE + first)

    def finish(self):
        ref = self.blocks(15)
        remote(ref, ref, self.send, self.recv.at[0], self.torus.device(0, 1, 0)).wait_send()


def near_side(i):
    return i + i // 2


def attend(query_ref, key_ref, value_ref, lengths_ref, keys, values, arrive, spread_q, fresh_kv, scores, mixed, out):
    factor = 1.0 / math.sqrt(128)
    spread_q[...] = jnp.zeros_like(spread_q)
    query = query_ref[...].astype(F32)
    fresh_kv[0] = key_ref[...].astype(F32)
    fresh_kv[1] = value_ref[...].astype(F32)
    for head in range(6):
        spread_q[:, head, :] = query[:, head * 128 : head * 128 + 128]
    position = lax.broadcasted_iota(jnp.int32, (8, 256), 1)

    def group(i, carry):
        some = pl.ds(i * 8, 8)
        arrive(0, i)
        for k in range(8):
            s = i * 8 + k
            raw = lax.dot_general(
                spread_q[s].astype(BF16),
                keys[s],
                (((1,), (1,)), ((), ())),
                preferred_element_type=F32,
            )
            scores[s] = jnp.where(position < lengths_ref[0, s], raw * factor, -jnp.inf)
        rows = pl.ds(pl.multiple_of(i * 8, 8), 8)
        fresh_key = fresh_kv[0, rows, :][:, None, :]
        fresh = jnp.sum(spread_q[some] * fresh_key, axis=-1, keepdims=True) * factor
        score = scores[some]
        highest = jnp.maximum(jnp.max(score, axis=-1, keepdims=True), fresh)
        weights = jnp.exp(score - highest)
        own = jnp.exp(fresh - highest)
        denominator = jnp.sum(weights, axis=-1, keepdims=True) + own
        probs = (weights / denominator).astype(BF16)
        own_prob = (own / denominator).astype(BF16).astype(F32)
        fresh_value = fresh_kv[1, rows, :][:, None, :]
        own_part = own_prob * fresh_value
        arrive(1, i)
        for k in range(8):
            s = i * 8 + k
            mixed[s] = jnp.dot(probs[k], values[s], preferred_element_type=F32) + own_part[k]
        return carry

    lax.fori_loop(0, 4, group, 0)
    for head in range(6):
        out[:, head * 128 : head * 128 + 128] = mixed[:, head, :].astype(BF16)


def layer(
    lengths_hbm,
    query_hbm,
    new_key_hbm,
    new_value_hbm,
    keys_hbm,
    values_hbm,
    proj_hbm,
    resid_hbm,
    gain_hbm,
    ids_hbm,
    gates_hbm,
    gate_hbm,
    up_hbm,
    down_hbm,
    stream_ref,
    mix_ref,
    lengths_ref,
    query,
    new_key,
    new_value,
    keys,
    values,
    spread_q,
    fresh_kv,
    scores,
    mixed,
    attn_mine,
    attn_all,
    proj,
    resid_ref,
    gain_ref,
    ids_ref,
    gates_ref,
    gate_w,
    up_w,
    down_w,
    heads,
    head_in,
    rows_all,
    gate_acc,
    up_acc,
    square_acc,
    hidden_all,
    down_acc,
    half_out,
    half_in,
    mix_part,
    mix_in,
    pick,
    place_t,
    weight_col,
    load_sem,
    cache_sem,
    attn_send,
    attn_recv,
    rows_send,
    rows_recv,
    hid_send,
    hid_recv,
    sib_send,
    sib_recv,
    swap_send,
    swap_recv,
    z_send,
    z_recv,
):
    role = lax.axis_index("role")
    grp = lax.axis_index("grp")
    plane = lax.axis_index("tp")
    x, y = grp // SIDE, lax.rem(grp, SIDE)
    torus = Torus(role, x, y, plane)
    sibling = (1 - role, grp, plane)

    def along_z(step):
        return (role, grp, lax.rem(plane + step, PLANES))

    barrier = pltpu.get_barrier_semaphore()
    near = [along_z(k) for k in FARTHEST_FIRST]
    near += [(role, lax.rem(x + k, SIDE) * SIDE + y, plane) for k in (2, 1, 3)]
    near += [(role, x * SIDE + lax.rem(y + k, SIDE), plane) for k in (2, 1, 3)]
    near += [sibling]
    for device in near:
        pl.semaphore_signal(barrier, inc=1, device_id=device, device_id_type=MESH)

    pairs = (
        (lengths_hbm, lengths_ref),
        (query_hbm, query),
        (new_key_hbm, new_key),
        (new_value_hbm, new_value),
        (ids_hbm, ids_ref),
        (gates_hbm, gates_ref),
        (gain_hbm, gain_ref),
        (proj_hbm, proj),
        (resid_hbm, resid_ref),
        (gate_hbm, gate_w),
        (up_hbm, up_w),
        (down_hbm, down_w),
    )
    loads = [pltpu.make_async_copy(src, dst, load_sem.at[i]) for i, (src, dst) in enumerate(pairs)]

    def cache_load(which, i):
        src, dst = ((keys_hbm, keys), (values_hbm, values))[which]
        some = pl.ds(i * 8, 8)
        return pltpu.make_async_copy(src.at[some], dst.at[some], cache_sem.at[which, i])

    for load in loads[:4]:
        load.start()
    for i in range(4):
        cache_load(0, i).start()
        cache_load(1, i).start()
    for load in loads[4:]:
        load.start()
    for load in loads[:4]:
        load.wait()
    attend(
        query,
        new_key,
        new_value,
        lengths_ref,
        keys,
        values,
        lambda which, i: cache_load(which, i).wait(),
        spread_q,
        fresh_kv,
        scores,
        mixed,
        attn_mine,
    )
    attn_all[pl.ds(grp * 32, 32), :] = attn_mine[...]
    pl.semaphore_wait(barrier, len(near))

    attn = PlaneGather(
        torus,
        lambda halves: attn_all.at[pl.ds(0, halves * 16)],
        lambda g, half: attn_all.at[pl.ds(g * 32 + half * 16, 16)],
        attn_send.at[0],
        attn_recv,
    )
    attn.start()

    for load in loads[4:9]:
        load.wait()
    ids = ids_ref[role]
    hit0, hit1 = ids[0:1, :] == plane, ids[1:2, :] == plane
    named = jnp.where(hit0 | hit1, 1.0, 0.0)
    gates = gates_ref[role]
    weight_row = jnp.where(hit0, gates[0:1, :], gates[1:2, :])
    seqs = named.shape[1]
    slots = pick.shape[0]
    earlier = lax.broadcasted_iota(jnp.int32, (seqs, seqs), 0) < lax.broadcasted_iota(
        jnp.int32, (seqs, seqs), 1
    )
    before = jnp.dot(
        jnp.broadcast_to(named, (16, seqs)).astype(BF16),
        jnp.where(earlier, 1.0, 0.0).astype(BF16),
        preferred_element_type=F32,
    )[0:1, :]
    slot = jnp.where(named > 0.5, before, -1.0).astype(jnp.int32)
    chosen = jnp.where(slot == lax.broadcasted_iota(jnp.int32, (slots, seqs), 0), 1.0, 0.0)
    pick[...] = chosen.astype(BF16)

    attn.forward()

    place_t[...] = chosen.T.astype(BF16)
    weight_col[...] = jnp.broadcast_to(
        jnp.sum(chosen * weight_row, axis=1, keepdims=True), weight_col.shape
    )
    gate_acc[...] = jnp.zeros_like(gate_acc)
    up_acc[...] = jnp.zeros_like(up_acc)
    square_acc[...] = jnp.zeros_like(square_acc)
    down_acc[...] = jnp.zeros_like(down_acc)

    mine = pl.ds(plane * 64, 64)

    def part_for(src, dst, s, step):
        to = lax.rem(plane + step, PLANES)
        sems = z_send.at[s], z_recv.at[s]
        return remote(src.at[pl.ds(to * 64, 64)], dst.at[step], *sems, along_z(step))

    def seven(ref, s):
        ref = ref.at[pl.ds(0, 7 * 64)]
        return remote(ref, ref, z_send.at[s], z_recv.at[s], along_z(1))

    def project(dx):
        row = lax.rem(x + dx, SIDE)
        some = pl.ds(row * 128, 128)
        part = jnp.dot(attn_all[some, :], proj[...], preferred_element_type=F32)
        heads[some, :] = part.astype(BF16)
        for k in range(2):
            step = lax.rem(2 * row + k + PLANES - plane, PLANES)

            @pl.when(step != 0)
            def _():
                part_for(heads, head_in, 0, step).start()

    attn.row(0, 3)
    project(0)

    def attn_rest(i, carry):
        dx = jnp.where(i == 2, 2, 2 * i + 1)
        attn.row(dx, 7)
        project(dx)
        return carry

    lax.fori_loop(0, 3, attn_rest, 0)

    def collect(src, dst, s):
        seven(src, s).wait_recv()

        def add(step, carry):
            return carry + dst[step].astype(F32)

        return lax.fori_loop(1, PLANES, add, src[mine, :].astype(F32))

    def spread(ref, s):
        block = ref.at[mine]
        for step in FARTHEST_FIRST:
            remote(block, block, z_send.at[s], z_recv.at[s], along_z(step)).start()
        seven(ref, s).wait_recv()

    summed = collect(heads, head_in, 0)
    stream_ref[mine, :] = (resid_ref[mine, :].astype(F32) + summed).astype(BF16)
    spread(stream_ref, 1)

    def gain_of(g):
        return jnp.concatenate([gain_ref[pl.ds(g * 3 + k, 1), :] for k in range(3)], axis=1)

    scaled = (stream_ref[...].astype(F32) * gain_of(grp)).astype(BF16)
    rows_all[role, grp] = jnp.dot(pick[...], scaled, preferred_element_type=F32).astype(BF16)
    rows = RelayGather(
        torus,
        lambda count: rows_all.at[role, pl.ds(0, count)],
        lambda g, half, part: rows_all.at[
            role, g, pl.ds(half * 128 + 64 * (part or 0), 128 if part is None else 64)
        ],
        rows_send.at[0],
        rows_recv,
    )
    rows.start()

    def block_at(dx, dy):
        return lax.rem(x + dx, SIDE) * SIDE + lax.rem(y + dy, SIDE)

    def share(group, dx, dy):
        block = rows_all.at[role, block_at(dx, dy)]
        remote(block, block, sib_send.at[0], sib_recv.at[group], sibling).start()

    def shared(group, count):
        ref = rows_all.at[1 - role, pl.ds(0, count)]
        remote(ref, ref, sib_send.at[0], sib_recv.at[group], sibling).wait_recv()

    def expert_in(dx, dy):
        g = block_at(dx, dy)
        depth = pl.ds(pl.multiple_of(g * 384, 128), 384)
        block = rows_all[:, g].reshape(512, 384)
        gate_acc[...] += jnp.dot(block, gate_w[depth, :], preferred_element_type=F32)
        up_acc[...] += jnp.dot(block, up_w[depth, :], preferred_element_type=F32)
        plain = block.astype(F32) * (1.0 / gain_of(g))
        plain = plain * plain
        square_acc[...] += plain[:, :128] + plain[:, 128:256] + plain[:, 256:]

    def beside(i):
        a = 1 + 2 * lax.rem(i, 2)
        return jnp.where(i < 2, a, 0), jnp.where(i < 2, 0, a)

    def across(i):
        return 1 + 2 * (i // 2), 1 + 2 * lax.rem(i, 2)

    def far(i):
        return (
            jnp.where(i < 3, 2, jnp.where(i < 6, near_side(i - 3), 2)),
            jnp.where(i < 3, near_side(i), 2),
        )

    def each(count, where, one):
        def body(i, carry):
            one(*where(i))
            return carry

        lax.fori_loop(0, count, body, 0)

    def share_all(group, count, where):
        each(count, where, lambda dx, dy: share(group, dx, dy))

    def enter(group, count, where):
        shared(group, count)
        each(count, where, expert_in)

    share(0, 0, 0)
    rows.turn()
    loads[9].wait()
    loads[10].wait()
    shared(0, 1)
    expert_in(0, 0)
    def far_pair(i, first):
        shared(3 + i, 2)
        expert_in(first, 2)
        expert_in(2, first)

    rows.relay(0)
    share_all(1, 4, beside)
    enter(1, 4, beside)
    rows.relay(1)
    share(2, 1, 1)
    rows.relay(3)
    share(2, 1, 3)
    share(2, 3, 1)
    share(2, 3, 3)
    rows.relay(2)
    for i, first in enumerate((0, 1, 3, 2)):
        rows.far(first)
        if first == 2:
            share(3 + i, 2, 2)
        else:
            share(3 + i, first, 2)
            share(3 + i, 2, first)
        if i == 0:
            enter(2, 4, across)
        else:
            far_pair(i - 1, (0, 1, 3)[i - 1])
    shared(6, 1)
    expert_in(2, 2)

    hid = RelayGather(
        torus,
        lambda count: hidden_all.at[pl.ds(0, count)],
        lambda g, half, part: hidden_all.at[
            g, pl.ds(half * 256 + 128 * (part or 0), 256 if part is None else 128)
        ],
        hid_send.at[0],
        hid_recv,
    )
    mean = jnp.sum(square_acc[...], axis=1, keepdims=True) / D
    rstat = 1.0 / jnp.sqrt(mean + 1e-05)
    act = gate_acc[...] * rstat
    hidden_all[grp] = (act / (1.0 + jnp.exp(-act)) * (up_acc[...] * rstat)).astype(BF16)
    hid.start()

    def expert_out(dx, dy):
        g = block_at(dx, dy)
        depth = pl.ds(pl.multiple_of(g * 256, 256), 256)
        down_acc[...] += jnp.dot(hidden_all[g], down_w[depth, :], preferred_element_type=F32)

    hid.turn()
    loads[11].wait()
    expert_out(0, 0)
    hid.relay(0)
    each(4, beside, expert_out)
    for first in (1, 3, 2):
        hid.relay(first)
    each(4, across, expert_out)
    hid.far(0)
    expert_out(0, 2)
    expert_out(2, 0)
    for first in (1, 3):
        hid.far(first)
        expert_out(first, 2)
        expert_out(2, first)
    hid.far(2)
    expert_out(2, 2)
    half_out[...] = down_acc[pl.ds((1 - role) * 256, 256), :].astype(BF16)
    swap = remote(half_out, half_in, swap_send.at[0], swap_recv.at[0], sibling)
    swap.start()

    swap.wait_recv()
    whole = down_acc[pl.ds(role * 256, 256), :] + half_in[...].astype(F32)
    weighted = (whole * weight_col[:, 0:1]).astype(BF16)
    mix_part[...] = jnp.dot(place_t[...], weighted, preferred_element_type=F32).astype(BF16)

    for step in FARTHEST_FIRST:
        part_for(mix_part, mix_in, 2, step).start()
    attn.finish()
    rows.finish()
    hid.finish()
    for i, ref in ((0, heads), (1, stream_ref)):
        seven(ref, i).wait_send()
    everything = rows_all.at[role]
    remote(everything, everything, sib_send.at[0], sib_recv.at[0], sibling).wait_send()
    mix_ref[mine, :] = collect(mix_part, mix_in, 2).astype(BF16)
    spread(mix_ref, 3)
    swap.wait_send()
    for i, ref in ((2, mix_part), (3, mix_ref)):
        seven(ref, i).wait_send()


def hand_over(stream_ref, mix_ref, stream_out, mix_out):
    stream_out[0] = stream_ref[...]
    mix_out[0] = mix_ref[...]


def local(
    queries,
    new_keys,
    new_values,
    cache_keys,
    cache_values,
    lengths,
    out_proj,
    residual,
    norm_gain,
    expert_ids,
    gate_weights,
    expert_gate,
    expert_up,
    expert_down,
):
    vmem = pl.BlockSpec(memory_space=pltpu.VMEM)
    hbm = pl.BlockSpec(memory_space=pl.ANY)
    dma = pltpu.SemaphoreType.DMA
    stream, mix = pl.pallas_call(
        layer,
        out_shape=(
            jax.ShapeDtypeStruct((512, 384), BF16),
            jax.ShapeDtypeStruct((512, 384), BF16),
        ),
        in_specs=[hbm] * 14,
        out_specs=(vmem, vmem),
        scratch_shapes=[
            pltpu.SMEM((1, 32), jnp.int32),
            pltpu.VMEM((32, 768), BF16),
            pltpu.VMEM((32, 128), BF16),
            pltpu.VMEM((32, 128), BF16),
            pltpu.VMEM((32, 256, 128), BF16),
            pltpu.VMEM((32, 256, 128), BF16),
            pltpu.VMEM((32, 8, 128), F32),
            pltpu.VMEM((2, 32, 128), F32),
            pltpu.VMEM((32, 8, 256), F32),
            pltpu.VMEM((32, 8, 128), F32),
            pltpu.VMEM((32, 768), BF16),
            pltpu.VMEM((512, 768), BF16),
            pltpu.VMEM((768, 384), BF16),
            pltpu.VMEM((512, 384), BF16),
            pltpu.VMEM((48, 128), F32),
            pltpu.VMEM((2, 2, 512), jnp.int32),
            pltpu.VMEM((2, 2, 512), F32),
            pltpu.VMEM((6144, 256), BF16),
            pltpu.VMEM((6144, 256), BF16),
            pltpu.VMEM((4096, 384), BF16),
            pltpu.VMEM((512, 384), BF16),
            pltpu.VMEM((8, 64, 384), BF16),
            pltpu.VMEM((2, 16, 256, 384), BF16),
            pltpu.VMEM((512, 256), F32),
            pltpu.VMEM((512, 256), F32),
            pltpu.VMEM((512, 128), F32),
            pltpu.VMEM((16, 512, 256), BF16),
            pltpu.VMEM((512, 384), F32),
            pltpu.VMEM((256, 384), BF16),
            pltpu.VMEM((256, 384), BF16),
            pltpu.VMEM((512, 384), BF16),
            pltpu.VMEM((8, 64, 384), BF16),
            pltpu.VMEM((256, 512), BF16),
            pltpu.VMEM((512, 256), BF16),
            pltpu.VMEM((256, 128), F32),
            dma((12,)),
            dma((2, 4)),
            dma((1,)),
            dma((12,)),
            dma((1,)),
            dma((16,)),
            dma((1,)),
            dma((16,)),
            dma((1,)),
            dma((7,)),
            dma((1,)),
            dma((1,)),
            dma((4,)),
            dma((4,)),
        ],
        compiler_params=pltpu.CompilerParams(
            collective_id=0, has_side_effects=True, vmem_limit_bytes=56 << 20
        ),
    )(
        lengths,
        queries[0],
        new_keys[0],
        new_values[0],
        cache_keys.reshape(32, 256, 128),
        cache_values.reshape(32, 256, 128),
        out_proj,
        residual[0],
        norm_gain.reshape(48, 128),
        jnp.swapaxes(expert_ids, 1, 2),
        jnp.swapaxes(gate_weights, 1, 2),
        expert_gate[0],
        expert_up[0],
        expert_down[0],
    )
    return pl.pallas_call(
        hand_over,
        out_shape=(jax.ShapeDtypeStruct((1, 512, 384), BF16),) * 2,
        in_specs=[vmem, vmem],
        out_specs=(vmem, vmem),
    )(stream, mix)


def solution(mesh):
    return jax.shard_map(
        local,
        mesh=mesh,
        in_specs=(
            P("role", "grp", "tp"),
            P("role", "grp", "tp"),
            P("role", "grp", "tp"),
            P("role", "grp", "tp", None, None),
            P("role", "grp", "tp", None, None),
            P("role", "grp"),
            P("tp", "grp"),
            P("role", None, "grp"),
            P(),
            P(),
            P(),
            P("tp", None, ("role", "grp")),
            P("tp", None, ("role", "grp")),
            P("tp", "role", "grp"),
        ),
        out_specs=(P("role", None, "grp"), P("role", None, "grp")),
        check_vma=False,
    )
```
